32 devices in a mesh: groups: 2 (over x), range: 16 (over z, y, core).
Axes of the slice: x: 2, y: 2, z: 4, core: 2. Of those that a mesh axis runs over, the one named last changes fastest.
Arguments:
- echoes: bfloat16 [4, 256, 16384], P('groups', 'range'), parts along dimension 0, may hold values from -6 to 6
- range_reference: float32 [2, 16384], replicated, may hold values from -6 to 6
- kernels: float32 [16, 8], replicated, may hold values from -2 to 2
- shifts: int32 [128, 256], P('range'), may hold values from 0 to 12
- phase_index: int32 [128, 256], P('range'), may hold values from 0 to 15
- centroid: int32 [128], P('range'), may hold values from 0 to 255
- azimuth_reference: float32 [2, 128, 256], P(None, 'range'), may hold values from -6 to 6
Outputs:
- focused_image: bfloat16 [4, 256, 16384], P('groups', None, 'range'), parts along dimension 0
The draws below stay inside these ranges and needn't reach their ends.
There are 2 independent parts, one for each index of `groups`. The reference program is written for one: setup_inputs(seed, part) draws one part's arguments, and reference() takes and returns one part's arrays. A program takes and returns all parts, laid end to end along the dimension named above; an argument that names none is the same for every part. Nothing has to cross between parts.
Inputs may be any that keep to these rules, and one draw needn't show every extreme that they name: `shifts`: whole range cells by which a block's energy at a Doppler bin has migrated. `phase_index`: row of kernels used by a block at a Doppler bin. `centroid`: doppler bins by which a block's azimuth reference is turned.
All inputs are finite; a program needn't handle non-finite values.
Results may differ from the reference program's by a relative error of at most 0.014.
Values may be sent and summed in bfloat16 or wider, within the bound.
A program may use at most 128 MiB of HBM per device.

```python
import math
import jax
import jax.numpy as jnp
from jax import lax

NR = 16384
P_DEV = 16
NA = 256
R1 = 128
RB = 128
NBLK = 128
PHASES = 16
TAPS = 8
MAXSHIFT = 12
HALO = 16
N_RANGE = 16


def place_ends(values, own_key, smallest, high):
    longest = values.shape.index(max(values.shape))
    spots = []
    for shift in (0, 1):
        where = [jax.random.randint(jax.random.fold_in(own_key, axis), (), 0, length) for axis, length in enumerate(values.shape)]
        where[longest] = (where[longest] + shift) % values.shape[longest]
        spots.append(tuple(where))
    return values.at[spots[0]].set(smallest).at[spots[1]].set(high)


def block_scale(stream_key, extent, cuts, least, high):
    gain = 1.0
    for position, shards_of in cuts:
        steps = jax.random.uniform(jax.random.fold_in(jax.random.fold_in(stream_key, 6), position), (shards_of,), jnp.float32, least / len(cuts), high / len(cuts))
        gain = gain * jnp.repeat(jnp.exp(steps), extent[position] // shards_of).reshape((-1,) + (1,) * (len(extent) - 1 - position))
    return gain


def centred(rng, shape, scale, bound, shards=(), held_as=jnp.bfloat16):
    drawn = jax.random.normal(rng, shape, jnp.float32) * scale
    if len(shards) > 0:
        drawn = block_scale(rng, shape, shards, -0.22, 0.18) * drawn
    return jnp.clip(drawn, min=-bound, max=bound).astype(held_as)


def setup_inputs(seed: int = 0, part: int = 0) -> dict:
    seeds = jax.random.split(jax.random.key(seed), 8)
    own_keys = jax.random.split(jax.random.fold_in(seeds[7], part), 8)
    echoes = centred(own_keys[0], (2, NA, NR), 1.0, 6.0, ((1, 16),))
    range_reference = centred(seeds[1], (2, NR), 1.0, 6.0, (), jnp.float32)
    kernels = centred(seeds[2], (PHASES, TAPS), 0.35, 2.0, (), jnp.float32)
    shifts = place_ends(jax.random.randint(seeds[3], (NBLK, NA), 0, MAXSHIFT + 1), jax.random.fold_in(seeds[3], 1), 0, MAXSHIFT).astype(jnp.int32)
    phase_index = place_ends(jax.random.randint(seeds[4], (NBLK, NA), 0, PHASES), jax.random.fold_in(seeds[4], 1), 0, PHASES - 1).astype(jnp.int32)
    centroid = place_ends(jax.random.randint(seeds[5], (NBLK,), 0, NA), jax.random.fold_in(seeds[5], 1), 0, NA - 1).astype(jnp.int32)
    azimuth_reference = centred(seeds[6], (2, NBLK, NA), 1.0, 6.0, ((1, 16),), jnp.float32)
    return dict(echoes=echoes, range_reference=range_reference, kernels=kernels, shifts=shifts, phase_index=phase_index, centroid=centroid, azimuth_reference=azimuth_reference)


def transform_matrix(length, orient):
    number_line = jnp.arange(length, dtype=jnp.int32)
    angles = 2.0 * math.pi / length * (number_line[:, None] * number_line[None, :] % length).astype(jnp.float32)
    cosine = jnp.cos(angles)
    sine_part = orient * jnp.sin(angles)
    matrix = jnp.stack([jnp.stack([cosine, -sine_part], 1), jnp.stack([sine_part, cosine], 1)], 0)
    return matrix.astype(jnp.bfloat16)

def twiddle(first_len, second_len, orient, factor):
    first_axis = jnp.arange(first_len, dtype=jnp.int32)
    second_axis = jnp.arange(second_len, dtype=jnp.int32)
    whole = first_len * second_len
    angles = 2.0 * math.pi / whole * (first_axis[:, None] * second_axis[None, :] % whole).astype(jnp.float32)
    return (jnp.cos(angles) * factor, orient * jnp.sin(angles) * factor)

def complex_times(values, real_part, imag_part):
    return jnp.stack([values[0] * real_part - values[1] * imag_part, values[0] * imag_part + values[1] * real_part], 0)

def product_of(pattern, matrix, values):
    return jnp.einsum(pattern, matrix.astype(jnp.float32), values.astype(jnp.float32), precision=lax.Precision.HIGHEST)

def range_lines(pulse_lines, reference_slots, range_first, range_second):
    values = pulse_lines.reshape(2, -1, range_first, range_second)
    twist_real, twist_imag = twiddle(range_first, range_second, -1.0, 1.0 / math.sqrt(range_first))
    halfway = complex_times(product_of('oaib,ipbm->opam', transform_matrix(range_first, -1.0), values), twist_real, twist_imag).astype(jnp.bfloat16)
    spectrum = product_of('oaib,ipkb->opka', transform_matrix(range_second, -1.0), halfway) * (1.0 / math.sqrt(range_second))
    spectrum = complex_times(spectrum, reference_slots[0], reference_slots[1]).astype(jnp.bfloat16)
    back_real, back_imag = twiddle(range_first, range_second, 1.0, 1.0 / math.sqrt(range_second))
    halfway = complex_times(product_of('oaib,ipkb->opka', transform_matrix(range_second, 1.0), spectrum), back_real, back_imag).astype(jnp.bfloat16)
    result = product_of('oaib,ipbm->opam', transform_matrix(range_first, 1.0), halfway) * (1.0 / math.sqrt(range_first))
    return result.reshape(2, -1, range_first * range_second).astype(jnp.bfloat16)

def azimuth_forward(cell_block, azimuth_first, azimuth_second):
    values = cell_block.reshape(2, azimuth_first, azimuth_second, -1)
    twist_real, twist_imag = twiddle(azimuth_first, azimuth_second, -1.0, 1.0 / math.sqrt(azimuth_first))
    halfway = complex_times(product_of('oaib,ibmc->oamc', transform_matrix(azimuth_first, -1.0), values), twist_real[:, :, None], twist_imag[:, :, None]).astype(jnp.bfloat16)
    spectrum = product_of('oaib,ikbc->okac', transform_matrix(azimuth_second, -1.0), halfway) * (1.0 / math.sqrt(azimuth_second))
    return spectrum.astype(jnp.bfloat16)

def azimuth_inverse(spectrum, azimuth_first, azimuth_second):
    back_real, back_imag = twiddle(azimuth_first, azimuth_second, 1.0, 1.0 / math.sqrt(azimuth_second))
    halfway = complex_times(product_of('oaib,ikbc->okac', transform_matrix(azimuth_second, 1.0), spectrum), back_real[:, :, None], back_imag[:, :, None]).astype(jnp.bfloat16)
    result = product_of('oaib,ibmc->oamc', transform_matrix(azimuth_first, 1.0), halfway) * (1.0 / math.sqrt(azimuth_first))
    return result.reshape(2, azimuth_first * azimuth_second, -1).astype(jnp.bfloat16)

def reference(echoes, range_reference, kernels, shifts, phase_index, centroid, azimuth_reference):
    range_first = R1
    range_second = NR // R1
    azimuth_first = N_RANGE
    azimuth_second = P_DEV
    lead_taps = TAPS // 2 - 1
    reference_slots = range_reference.reshape(2, range_second, range_first).transpose(0, 2, 1)
    groups = echoes.reshape(2, azimuth_first, azimuth_second, NR).transpose(1, 0, 2, 3)
    compressed = lax.map(lambda pulse_lines: range_lines(pulse_lines, reference_slots, range_first, range_second), groups)
    compressed = compressed.transpose(1, 0, 2, 3).reshape(2, NA, NR)
    cell_blocks = compressed.reshape(2, NA, NBLK, RB).transpose(2, 0, 1, 3)
    spectra = lax.map(lambda cell_block: azimuth_forward(cell_block, azimuth_first, azimuth_second).reshape(2, NA, RB), cell_blocks)
    doppler = spectra.transpose(1, 2, 0, 3).reshape(2, NA, NR)
    padded = jnp.pad(doppler, ((0, 0), (0, 0), (HALO, HALO)))
    bin_of_slot = (jnp.arange(azimuth_first, dtype=jnp.int32)[:, None] + azimuth_first * jnp.arange(azimuth_second, dtype=jnp.int32)[None, :]).reshape(NA)
    cell_line = jnp.arange(RB, dtype=jnp.int32)

    def focus(block_index):
        window = lax.dynamic_slice_in_dim(padded, (block_index * RB).astype(jnp.int32), RB + 2 * HALO, 2)
        shift_rows = shifts[block_index][bin_of_slot]
        phase_rows = phase_index[block_index][bin_of_slot]
        weights = kernels[phase_rows]
        summed = jnp.zeros((2, NA, RB), jnp.float32)
        for tap_index in range(TAPS):
            where_from = (HALO - lead_taps + tap_index + cell_line[None, :] + shift_rows[:, None]).astype(jnp.int32)
            picked = jnp.take_along_axis(window, jnp.broadcast_to(where_from[None], (2, NA, RB)), axis=2)
            summed = summed + weights[:, tap_index][None, :, None] * picked.astype(jnp.float32)
        rolled = azimuth_reference[:, block_index][:, ((bin_of_slot - centroid[block_index]) % NA).astype(jnp.int32)]
        focused = complex_times(summed, rolled[0][:, None], rolled[1][:, None]).astype(jnp.bfloat16)
        return azimuth_inverse(focused.reshape(2, azimuth_first, azimuth_second, RB), azimuth_first, azimuth_second)
    images = lax.map(focus, jnp.arange(NBLK, dtype=jnp.int32))
    return images.transpose(1, 2, 0, 3).reshape(2, NA, NR)
```

```python
import functools
import math

import jax
import jax.numpy as jnp
import ml_dtypes
import numpy as np
from jax import lax
from jax.experimental import pallas as pl
from jax.experimental.pallas import tpu as pltpu
from jax.sharding import PartitionSpec as P

R1 = 128
RB = 128
F32 = jnp.float32
BF16 = jnp.bfloat16


def roots(length, orient):
    line = np.arange(length)
    angles = 2.0 * math.pi / length * (line[:, None] * line[None, :] % length)
    rounded = lambda part: part.astype(ml_dtypes.bfloat16).astype(np.float64)
    return rounded(np.cos(angles)) + 1j * orient * rounded(np.sin(angles))


def twist(first_len, second_len, orient):
    whole = first_len * second_len
    turns = np.arange(first_len)[:, None] * np.arange(second_len)[None, :] % whole
    return np.exp(orient * 2j * math.pi / whole * turns)


def left_matrix(m):
    return np.block([[m.real, -m.imag], [m.imag, m.real]]).astype(ml_dtypes.bfloat16)


def right_matrix(m):
    return np.block([[m.real, m.imag], [-m.imag, m.real]]).astype(ml_dtypes.bfloat16)


def pair(m):
    return np.stack([m.real, m.imag]).astype(np.float32)


def azimuth_matrix(first, second):
    parts = np.einsum(
        "ka,mk,bm->bkam", roots(first, -1.0), twist(second, first, -1.0), roots(second, -1.0)
    )
    return parts.reshape(first * second, first * second) / math.sqrt(first * second)


def dot(a, b):
    return jnp.dot(a, b, preferred_element_type=F32)


def range_kernel(
    ranks, e_ref, ref_ref, first_ref, second_ref, back2_ref, back1_ref, tw_ref, bw_ref,
    send_ref, lines, cells, slots,
):
    pulses = e_ref.shape[1]
    blocks = R1 // ranks
    for part in range(2):
        slots[part] = ref_ref[part].T

    def spread(n1, carry):
        lane = pl.multiple_of(n1 * RB, RB)
        for part in range(2):
            lines[part, pl.ds(n1, pulses, stride=R1), :] = e_ref[part, :, pl.ds(lane, RB)].astype(F32)
        return carry

    lax.fori_loop(0, R1, spread, 0, unroll=8)

    def times(re, im, table):
        tr, ti = table[0], table[1]
        return re * tr - im * ti, re * ti + im * tr

    def step(p, carry):
        row = pl.multiple_of(p * R1, R1)
        x = jnp.concatenate([lines[0, pl.ds(row, R1), :], lines[1, pl.ds(row, R1), :]], 0).astype(BF16)
        u = dot(first_ref[...], x)
        ur, ui = times(u[:R1], u[R1:], tw_ref)
        u = jnp.concatenate([ur.astype(BF16), ui.astype(BF16)], 1)
        s = dot(u, second_ref[...])
        sr, si = times(s[:, :RB], s[:, RB:], slots)
        s = jnp.concatenate([sr.astype(BF16), si.astype(BF16)], 1)
        v = dot(s, back2_ref[...])
        vr, vi = times(v[:, :RB], v[:, RB:], bw_ref)
        v = jnp.concatenate([vr.astype(BF16), vi.astype(BF16)], 0)
        r = dot(back1_ref[...], v)
        cells[0, pl.ds(p, R1, stride=pulses), :] = r[:R1]
        cells[1, pl.ds(p, R1, stride=pulses), :] = r[R1:]
        return carry

    lax.fori_loop(0, pulses, step, 0, unroll=2)

    span = blocks * pulses
    lane = lax.broadcasted_iota(jnp.int32, (pulses, RB), 1)

    for d in range(ranks):
        for part in range(2):
            send_ref[d, part * span : (part + 1) * span, :] = cells[
                part, d * span : (d + 1) * span, :
            ].astype(BF16)
        packed = []
        for part in range(2):
            zero = jnp.zeros((pulses, RB), F32)
            after = zero if d == ranks - 1 else cells[part, (d + 1) * span : (d + 1) * span + pulses, :]
            before = zero if d == 0 else cells[part, d * span - pulses : d * span, :]
            packed.append(jnp.where(lane < RB // 2, after, before))
        mine = (lane < RB // 4) | (lane >= RB - RB // 4)
        send_ref[d, 2 * span :, :] = jnp.where(
            mine, packed[0], pltpu.roll(packed[1], RB // 2, 1)
        ).astype(BF16)


def azimuth_kernel(
    got_ref, kernels_ref, shift_ref, phase_ref, centroid_ref, az_ref, ahead_ref, back_ref,
    out_ref, doppler, columns,
):
    ranks = got_ref.shape[0]
    blocks, total = shift_ref.shape
    pulses = total // ranks
    taps = kernels_ref.shape[1]
    lead = taps // 2 - 1
    span = blocks * pulses
    rows = []
    for part in range(2):
        for b in range(blocks):
            rows.append(pltpu.roll(az_ref[part, b : b + 1, :], centroid_ref[b], 1))
    rows.append(shift_ref[...].astype(F32))
    rows.append(phase_ref[...].astype(F32))
    rows.append(jnp.zeros((RB - 4 * blocks, total), F32))
    columns[...] = jnp.concatenate(rows, 0).T
    table = jnp.concatenate([kernels_ref[...].T, jnp.zeros((taps, RB - kernels_ref.shape[0]), F32)], 1)

    def gather(tile, part, b):
        begin = (part * blocks + b) * pulses
        return tile[:, begin : begin + pulses, :].reshape(total, RB)

    for b in range(blocks):
        x = jnp.concatenate([gather(got_ref, 0, b), gather(got_ref, 1, b)], 0)
        doppler[b + 1] = dot(ahead_ref[...], x)
    halo = got_ref[:, 2 * span :, :].reshape(total, RB)
    turned = jnp.concatenate([halo[:, RB // 2 :], halo[:, : RB // 2]], 1)
    edge = dot(ahead_ref[...], jnp.concatenate([halo, turned], 0))
    doppler[0] = edge
    doppler[blocks + 1] = edge

    size = 16
    lane = lax.broadcasted_iota(jnp.int32, (size, RB), 1)

    for b in range(blocks):

        def some(i, carry):
            row = pl.multiple_of(i * size, size)

            def column(j):
                at = columns[pl.ds(row, size), j : j + 1]
                return jnp.broadcast_to(at, (size, RB))

            shift = column(2 * blocks + b).astype(jnp.int32)
            phase = column(3 * blocks + b).astype(jnp.int32)
            weights = [
                jnp.take_along_axis(
                    jnp.broadcast_to(table[t : t + 1], (size, RB)), phase, axis=1
                )
                for t in range(taps)
            ]
            where = (lane + shift + (RB - lead)) & (RB - 1)
            early = lane < RB - shift
            found = []
            for part in range(2):
                at = pl.ds(part * total + row, size)
                prev, cur, after = doppler[b, at, :], doppler[b + 1, at, :], doppler[b + 2, at, :]
                a = jnp.take_along_axis(jnp.where(lane >= RB - lead, prev, cur), where, axis=1)
                z = jnp.take_along_axis(jnp.where(lane >= RB - lead, cur, after), where, axis=1)
                x = jnp.where(early, a, z)
                total_sum = weights[0] * x
                for t in range(1, taps):
                    total_sum += weights[t] * pltpu.roll(jnp.where(lane < t, z, x), RB - t, 1)
                found.append(total_sum)
            ar, ai = column(b), column(blocks + b)
            re = found[0] * ar - found[1] * ai
            im = found[0] * ai + found[1] * ar
            doppler[b, pl.ds(row, size), :] = re
            doppler[b, pl.ds(total + row, size), :] = im
            return carry

        lax.fori_loop(0, total // size, some, 0)
        y = dot(back_ref[...], doppler[b].astype(BF16)).astype(BF16)
        out_ref[0, :, b * RB : (b + 1) * RB] = y[:total]
        out_ref[1, :, b * RB : (b + 1) * RB] = y[total:]


def local(echoes, range_reference, kernels, shifts, phase_index, centroid, azimuth_reference):
    ranks = lax.axis_size("range")
    pulses, samples = echoes.shape[1:]
    second = samples // R1
    blocks = R1 // ranks
    total = ranks * pulses
    fft1 = left_matrix(roots(R1, -1.0))
    fft2 = right_matrix(roots(second, -1.0))
    inv2 = right_matrix(roots(second, 1.0))
    inv1 = left_matrix(roots(R1, 1.0))
    ahead_twist = pair(twist(R1, second, -1.0) / math.sqrt(samples))
    back_twist = pair(twist(R1, second, 1.0) / math.sqrt(samples))
    turn = azimuth_matrix(ranks, pulses)
    vmem = pl.BlockSpec(memory_space=pltpu.VMEM)
    height = 2 * blocks * pulses + pulses
    send = pl.pallas_call(
        functools.partial(range_kernel, ranks),
        out_shape=jax.ShapeDtypeStruct((ranks, height, RB), BF16),
        in_specs=[vmem] * 8,
        out_specs=vmem,
        scratch_shapes=[
            pltpu.VMEM((2, R1 * pulses, RB), F32),
            pltpu.VMEM((2, R1 * pulses, RB), F32),
            pltpu.VMEM((2, R1, second), F32),
        ],
        compiler_params=pltpu.CompilerParams(vmem_limit_bytes=40 << 20),
        name="range_lines",
    )(
        echoes, range_reference.reshape(2, second, R1), fft1, fft2, inv2, inv1, ahead_twist, back_twist,
    )
    got = lax.all_to_all(send, "range", split_axis=0, concat_axis=0, tiled=True)
    return pl.pallas_call(
        azimuth_kernel,
        out_shape=jax.ShapeDtypeStruct((2, total, blocks * RB), BF16),
        in_specs=[vmem] * 4 + [pl.BlockSpec(memory_space=pltpu.SMEM)] + [vmem] * 3,
        out_specs=vmem,
        scratch_shapes=[
            pltpu.VMEM((blocks + 2, 2 * total, RB), F32),
            pltpu.VMEM((total, RB), F32),
        ],
        compiler_params=pltpu.CompilerParams(vmem_limit_bytes=48 << 20),
        name="azimuth",
    )(
        got, kernels, shifts, phase_index, centroid, azimuth_reference,
        left_matrix(turn), left_matrix(turn.conj().T),
    )


def solution(mesh):
    in_specs = (
        P("groups", "range", None),
        P(),
        P(),
        P("range", None),
        P("range", None),
        P("range"),
        P(None, "range", None),
    )
    out_specs = P("groups", None, "range")
    return jax.shard_map(local, mesh=mesh, in_specs=in_specs, out_specs=out_specs, check_vma=False)
```

```python
import functools
import math

import jax
import jax.numpy as jnp
import ml_dtypes
import numpy as np
from jax import lax
from jax.experimental import pallas as pl
from jax.experimental.pallas import tpu as pltpu
from jax.sharding import PartitionSpec as P

R1 = 128
RB = 128
F32 = jnp.float32
BF16 = jnp.bfloat16
VMEM_BYTES = 58 << 20


def roots(length, orient):
    line = np.arange(length)
    angles = 2.0 * math.pi / length * (line[:, None] * line[None, :] % length)
    rounded = lambda part: part.astype(ml_dtypes.bfloat16).astype(np.float64)
    return rounded(np.cos(angles)) + 1j * orient * rounded(np.sin(angles))


def twist(first_len, second_len, orient):
    whole = first_len * second_len
    turns = np.arange(first_len)[:, None] * np.arange(second_len)[None, :] % whole
    return np.exp(orient * 2j * math.pi / whole * turns)


def left_matrix(m):
    return np.block([[m.real, -m.imag], [m.imag, m.real]]).astype(ml_dtypes.bfloat16)


def right_matrix(m):
    return np.block([[m.real, m.imag], [-m.imag, m.real]]).astype(ml_dtypes.bfloat16)


def pair(m):
    return np.stack([m.real, m.imag]).astype(np.float32)


def azimuth_matrix(first, second):
    parts = np.einsum(
        "ka,mk,bm->bkam", roots(first, -1.0), twist(second, first, -1.0), roots(second, -1.0)
    )
    return parts.reshape(first * second, first * second) / math.sqrt(first * second)


def dot(a, b):
    return jnp.dot(a, b, preferred_element_type=F32)


def fetch(pairs, sems):
    copies = [pltpu.make_async_copy(src, dst, sems.at[i]) for i, (src, dst) in enumerate(pairs)]
    for copy in copies:
        copy.start()
    return copies


def range_kernel(
    ranks, group, e_hbm, ref_hbm, mats_hbm, tables_hbm, send_ref,
    lines, cells, slots, e_ref, ref_ref, mats, tables, sems,
):
    pulses = e_ref.shape[1]
    blocks = R1 // ranks
    copies = fetch(
        [(e_hbm, e_ref), (ref_hbm, ref_ref), (tables_hbm, tables), (mats_hbm, mats)], sems
    )
    copies[0].wait()

    def spread(n1, carry):
        lane = pl.multiple_of(n1 * RB, RB)
        for part in range(2):
            lines[part, pl.ds(n1, pulses, stride=R1), :] = e_ref[part, :, pl.ds(lane, RB)].astype(F32)
        return carry

    lax.fori_loop(0, R1, spread, 0, unroll=8)
    for copy in copies[1:]:
        copy.wait()
    for part in range(2):
        for k2 in range(ref_ref.shape[1] // R1):
            slots[part, k2 : k2 + 1, :] = ref_ref[part : part + 1, k2 * R1 : (k2 + 1) * R1]
    for part in range(2):
        slots[part] = slots[part].T

    def times(re, im, tr, ti):
        return (re * tr - im * ti).astype(BF16), (re * ti + im * tr).astype(BF16)

    def step(g, carry):
        def line(part, j):
            return lines[part, pl.ds(pl.multiple_of((g * group + j) * R1, R1), R1), :].astype(BF16)

        x = jnp.concatenate(
            [jnp.concatenate([line(part, j) for j in range(group)], 1) for part in range(2)], 0
        )
        u = dot(mats[0], x)
        tr, ti = tables[0], tables[1]
        u = jnp.concatenate(
            [
                jnp.concatenate(
                    times(u[:R1, j * RB : (j + 1) * RB], u[R1:, j * RB : (j + 1) * RB], tr, ti), 1
                )
                for j in range(group)
            ],
            0,
        )
        s = dot(u, mats[1])
        tr, ti = slots[0], slots[1]
        s = jnp.concatenate(
            [
                jnp.concatenate(
                    times(s[j * R1 : (j + 1) * R1, :RB], s[j * R1 : (j + 1) * R1, RB:], tr, ti), 1
                )
                for j in range(group)
            ],
            0,
        )
        v = dot(s, mats[2])
        tr, ti = tables[2], tables[3]
        v = jnp.concatenate(
            [
                jnp.concatenate(
                    times(v[j * R1 : (j + 1) * R1, :RB], v[j * R1 : (j + 1) * R1, RB:], tr, ti), 0
                )
                for j in range(group)
            ],
            1,
        )
        r = dot(mats[3], v)
        for j in range(group):
            for part in range(2):
                cells[part, pl.ds(g * group + j, R1, stride=pulses), :] = r[
                    part * R1 : (part + 1) * R1, j * RB : (j + 1) * RB
                ]
        return carry

    lax.fori_loop(0, pulses // group, step, 0)

    lane = lax.broadcasted_iota(jnp.int32, (pulses, RB), 1)
    mine = (lane < RB // 4) | (lane >= RB - RB // 4)
    zero = jnp.zeros((pulses, RB), F32)

    for d in range(ranks):
        packed = []
        for part in range(2):
            after = zero if d == ranks - 1 else cells[part, pl.ds((d + 1) * blocks * pulses, pulses), :]
            before = zero if d == 0 else cells[part, pl.ds((d * blocks - 1) * pulses, pulses), :]
            packed.append(jnp.where(lane < RB // 2, after, before))
        send_ref[d, :pulses, :] = jnp.where(
            mine, packed[0], pltpu.roll(packed[1], RB // 2, 1)
        ).astype(BF16)
        for b in range(blocks):
            for part in range(2):
                begin = pulses + (2 * b + part) * pulses
                send_ref[d, begin : begin + pulses, :] = cells[
                    part, pl.ds((d * blocks + b) * pulses, pulses), :
                ].astype(BF16)


def turn_kernel(
    ranks, chunk, send_hbm, kernels_hbm, shift_hbm, phase_hbm, az_hbm, ahead_hbm, back_hbm, centroid_ref,
    out_ref, got, doppler, columns, weights, filters, moves,
    kernels_ref, shift_ref, phase_ref, az_ref, ahead, back, sems, send_sems, got_sems,
):
    me = lax.axis_index("range")
    blocks, total = shift_ref.shape
    pulses = total // ranks
    taps = kernels_ref.shape[1]
    lead = taps // 2 - 1
    chunks = blocks // chunk

    barrier = pltpu.get_barrier_semaphore()

    def greet(k, carry):
        pl.semaphore_signal(
            barrier, inc=1, device_id={"range": lax.rem(me + k, ranks)},
            device_id_type=pl.DeviceIdType.MESH,
        )
        return carry

    lax.fori_loop(1, ranks, greet, 0)
    copies = fetch(
        [
            (kernels_hbm, kernels_ref), (shift_hbm, shift_ref), (phase_hbm, phase_ref),
            (az_hbm, az_ref), (ahead_hbm, ahead), (back_hbm, back), (send_hbm.at[me], got.at[me]),
        ],
        sems,
    )
    pl.semaphore_wait(barrier, ranks - 1)

    def rows(c):
        if c == 0:
            return pl.ds(0, pulses + 2 * chunk * pulses)
        return pl.ds(pulses + 2 * c * chunk * pulses, 2 * chunk * pulses)

    def remote(c, to, owner):
        return pltpu.make_async_remote_copy(
            src_ref=send_hbm.at[to, rows(c)],
            dst_ref=got.at[owner, rows(c)],
            send_sem=send_sems.at[c, to],
            recv_sem=got_sems.at[c, owner],
            device_id={"range": to},
            device_id_type=pl.DeviceIdType.MESH,
        )

    half = ranks // 2
    for c in range(chunks):

        def begin(k, carry):
            remote(c, lax.rem(me + k, ranks), me).start()
            return carry

        lax.fori_loop(half, ranks, begin, 0)
        lax.fori_loop(1, half, begin, 0)

    for copy in copies:
        copy.wait()

    wide = lax.broadcasted_iota(jnp.int32, (blocks, 1), 0)
    turns = jnp.zeros((blocks, 1), jnp.int32)
    for b in range(blocks):
        turns = jnp.where(wide == b, centroid_ref[b], turns)
    turns = jnp.broadcast_to(turns, (blocks, total))
    lines = []
    for part in range(2):
        line = az_ref[part]
        step = 1
        while step < total:
            line = jnp.where((turns & step) != 0, pltpu.roll(line, step, 1), line)
            step *= 2
        lines.append(line)
    lines.append(shift_ref[...].astype(F32))
    lines.append(phase_ref[...].astype(F32))
    lines.append(jnp.zeros((RB - 4 * blocks, total), F32))
    columns[...] = jnp.concatenate(lines, 0).T
    table = jnp.concatenate([kernels_ref[...].T, jnp.zeros((taps, RB - kernels_ref.shape[0]), F32)], 1)

    def prepare(i, carry):
        row = pl.ds(pl.multiple_of(i * 8, 8), 8)
        tile = columns[row, :]
        tables = [jnp.broadcast_to(table[t : t + 1], (8, RB)) for t in range(taps)]

        def column(j):
            return jnp.broadcast_to(tile[:, j : j + 1], (8, RB))

        for b in range(blocks):
            filters[b, 0, row, :] = column(b)
            filters[b, 1, row, :] = column(blocks + b)
            moves[b, row, :] = column(2 * blocks + b).astype(jnp.int32)
            phase = column(3 * blocks + b).astype(jnp.int32)
            for t in range(taps):
                weights[b, t, row, :] = jnp.take_along_axis(tables[t], phase, axis=1)
        return carry

    lax.fori_loop(0, total // 8, prepare, 0)

    size = 32
    lane = lax.broadcasted_iota(jnp.int32, (size, RB), 1)

    def focus(b):
        def some(i, carry):
            row = pl.multiple_of(i * size, size)
            here = pl.ds(row, size)
            shift = moves[b, here, :]
            where = (lane + shift + (RB - lead)) & (RB - 1)
            early = lane < RB - shift
            found = []
            for part in range(2):
                at = pl.ds(part * total + row, size)
                prev, cur, after = doppler[b, at, :], doppler[b + 1, at, :], doppler[b + 2, at, :]
                a = jnp.take_along_axis(jnp.where(lane >= RB - lead, prev, cur), where, axis=1)
                z = jnp.take_along_axis(jnp.where(lane >= RB - lead, cur, after), where, axis=1)
                x = jnp.where(early, a, z)
                summed = weights[b, 0, here, :] * x
                for t in range(1, taps):
                    summed += weights[b, t, here, :] * pltpu.roll(jnp.where(lane < t, z, x), RB - t, 1)
                found.append(summed)
            ar, ai = filters[b, 0, here, :], filters[b, 1, here, :]
            doppler[b, here, :] = found[0] * ar - found[1] * ai
            doppler[b, pl.ds(total + row, size), :] = found[0] * ai + found[1] * ar
            return carry

        lax.fori_loop(0, total // size, some, 0)
        y = dot(back[...], doppler[b].astype(BF16)).astype(BF16)
        out_ref[0, :, b * RB : (b + 1) * RB] = y[:total]
        out_ref[1, :, b * RB : (b + 1) * RB] = y[total:]

    for c in range(chunks):

        def arrive(k, carry):
            remote(c, me, lax.rem(me + k, ranks)).wait_recv()
            return carry

        lax.fori_loop(1, ranks, arrive, 0)
        if c == 0:
            halo = got[:, :pulses, :]
            turned = jnp.concatenate([halo[:, :, RB // 2 :], halo[:, :, : RB // 2]], 2)
            edge = jnp.stack([halo, turned], 1).reshape(2 * total, RB)
            edge = dot(ahead[...], edge)
            doppler[0] = edge
            doppler[blocks + 1] = edge
        for b in range(c * chunk, (c + 1) * chunk):
            begin_row = pulses + 2 * b * pulses
            x = got[:, begin_row : begin_row + 2 * pulses, :].reshape(2 * total, RB)
            doppler[b + 1] = dot(ahead[...], x)
        for b in range(max(c * chunk - 1, 0), (c + 1) * chunk - (c < chunks - 1)):
            focus(b)

    for c in range(chunks):

        def leave(k, carry):
            remote(c, lax.rem(me + k, ranks), me).wait_send()
            return carry

        lax.fori_loop(1, ranks, leave, 0)


def local(echoes, range_reference, kernels, shifts, phase_index, centroid, azimuth_reference):
    ranks = lax.axis_size("range")
    pulses, samples = echoes.shape[1:]
    second = samples // R1
    blocks = R1 // ranks
    total = ranks * pulses
    taps = kernels.shape[1]
    mats = np.stack([
        left_matrix(roots(R1, -1.0)),
        right_matrix(roots(second, -1.0)),
        right_matrix(roots(second, 1.0)),
        left_matrix(roots(R1, 1.0)),
    ])
    tables = np.concatenate([
        pair(twist(R1, second, -1.0) / math.sqrt(samples)),
        pair(twist(R1, second, 1.0) / math.sqrt(samples)),
    ])
    turn = azimuth_matrix(ranks, pulses)
    ahead = left_matrix(turn).reshape(2 * total, 2, ranks, pulses).transpose(0, 2, 1, 3)
    ahead = ahead.reshape(2 * total, 2 * total)
    back = left_matrix(turn.conj().T)
    vmem = pl.BlockSpec(memory_space=pltpu.VMEM)
    anywhere = pl.BlockSpec(memory_space=pl.ANY)
    height = 2 * blocks * pulses + pulses
    dma = pltpu.SemaphoreType.DMA
    send = pl.pallas_call(
        functools.partial(range_kernel, ranks, math.gcd(pulses, 4)),
        out_shape=jax.ShapeDtypeStruct((ranks, height, RB), BF16),
        in_specs=[anywhere] * 4,
        out_specs=vmem,
        scratch_shapes=[
            pltpu.VMEM((2, R1 * pulses, RB), F32),
            pltpu.VMEM((2, R1 * pulses, RB), F32),
            pltpu.VMEM((2, R1, second), F32),
            pltpu.VMEM(echoes.shape, BF16),
            pltpu.VMEM(range_reference.shape, F32),
            pltpu.VMEM(mats.shape, BF16),
            pltpu.VMEM(tables.shape, F32),
            dma((4,)),
        ],
        compiler_params=pltpu.CompilerParams(vmem_limit_bytes=VMEM_BYTES),
        name="range_lines",
    )(echoes, range_reference, mats, tables)
    chunk = max(1, blocks // 4)
    return pl.pallas_call(
        functools.partial(turn_kernel, ranks, chunk),
        out_shape=jax.ShapeDtypeStruct((2, total, blocks * RB), BF16),
        in_specs=[anywhere] * 7 + [pl.BlockSpec(memory_space=pltpu.SMEM)],
        out_specs=vmem,
        scratch_shapes=[
            pltpu.VMEM((ranks, height, RB), BF16),
            pltpu.VMEM((blocks + 2, 2 * total, RB), F32),
            pltpu.VMEM((total, RB), F32),
            pltpu.VMEM((blocks, taps, total, RB), F32),
            pltpu.VMEM((blocks, 2, total, RB), F32),
            pltpu.VMEM((blocks, total, RB), jnp.int32),
            pltpu.VMEM(kernels.shape, F32),
            pltpu.VMEM(shifts.shape, jnp.int32),
            pltpu.VMEM(shifts.shape, jnp.int32),
            pltpu.VMEM(azimuth_reference.shape, F32),
            pltpu.VMEM(ahead.shape, BF16),
            pltpu.VMEM(back.shape, BF16),
            dma((7,)),
            dma((blocks // chunk, ranks)),
            dma((blocks // chunk, ranks)),
        ],
        compiler_params=pltpu.CompilerParams(
            vmem_limit_bytes=VMEM_BYTES, collective_id=0, has_side_effects=True
        ),
        name="turn_and_azimuth",
    )(send, kernels, shifts, phase_index, azimuth_reference, ahead, back, centroid)


def solution(mesh):
    in_specs = (
        P("groups", "range", None),
        P(),
        P(),
        P("range", None),
        P("range", None),
        P("range"),
        P(None, "range", None),
    )
    out_specs = P("groups", None, "range")
    return jax.shard_map(local, mesh=mesh, in_specs=in_specs, out_specs=out_specs, check_vma=False)
```

```python
import functools
import math

import jax
import jax.numpy as jnp
import ml_dtypes
import numpy as np
from jax import lax
from jax.experimental import pallas as pl
from jax.experimental.pallas import tpu as pltpu
from jax.sharding import PartitionSpec as P

R1 = 128
RB = 128
F32 = jnp.float32
BF16 = jnp.bfloat16
VMEM_BYTES = 58 << 20


def roots(length, orient):
    line = np.arange(length)
    angles = 2.0 * math.pi / length * (line[:, None] * line[None, :] % length)
    rounded = lambda part: part.astype(ml_dtypes.bfloat16).astype(np.float64)
    return rounded(np.cos(angles)) + 1j * orient * rounded(np.sin(angles))


def twist(first_len, second_len, orient):
    whole = first_len * second_len
    turns = np.arange(first_len)[:, None] * np.arange(second_len)[None, :] % whole
    return np.exp(orient * 2j * math.pi / whole * turns)


def left_matrix(m):
    return np.block([[m.real, -m.imag], [m.imag, m.real]]).astype(ml_dtypes.bfloat16)


def right_matrix(m):
    return np.block([[m.real, m.imag], [-m.imag, m.real]]).astype(ml_dtypes.bfloat16)


def pair(m):
    return np.stack([m.real, m.imag]).astype(np.float32)


def azimuth_matrix(first, second):
    parts = np.einsum(
        "ka,mk,bm->bkam", roots(first, -1.0), twist(second, first, -1.0), roots(second, -1.0)
    )
    return parts.reshape(first * second, first * second) / math.sqrt(first * second)


def dot(a, b):
    return jnp.dot(a, b, preferred_element_type=F32)


def fetch(pairs, sems):
    copies = [pltpu.make_async_copy(src, dst, sems.at[i]) for i, (src, dst) in enumerate(pairs)]
    for copy in copies:
        copy.start()
    return copies


def range_kernel(
    ranks, group, e_hbm, ref_hbm, mats_hbm, tables_hbm, send_ref,
    lines, cells, slots, e_ref, ref_ref, mats, tables, sems,
):
    pulses = e_ref.shape[1]
    blocks = R1 // ranks
    copies = fetch(
        [(e_hbm, e_ref), (ref_hbm, ref_ref), (tables_hbm, tables), (mats_hbm, mats)], sems
    )
    copies[0].wait()

    def spread(n1, carry):
        lane = pl.multiple_of(n1 * RB, RB)
        for part in range(2):
            lines[part, pl.ds(n1, pulses, stride=R1), :] = e_ref[part, :, pl.ds(lane, RB)].astype(F32)
        return carry

    lax.fori_loop(0, R1, spread, 0, unroll=8)
    for copy in copies[1:]:
        copy.wait()
    for part in range(2):
        for k2 in range(ref_ref.shape[1] // R1):
            slots[part, k2 : k2 + 1, :] = ref_ref[part : part + 1, k2 * R1 : (k2 + 1) * R1]
    for part in range(2):
        slots[part] = slots[part].T

    def times(re, im, tr, ti):
        return (re * tr - im * ti).astype(BF16), (re * ti + im * tr).astype(BF16)

    def step(g, carry):
        def line(part, j):
            return lines[part, pl.ds(pl.multiple_of((g * group + j) * R1, R1), R1), :].astype(BF16)

        x = jnp.concatenate(
            [jnp.concatenate([line(part, j) for j in range(group)], 1) for part in range(2)], 0
        )
        u = dot(mats[0], x)
        tr, ti = tables[0], tables[1]
        u = jnp.concatenate(
            [
                jnp.concatenate(
                    times(u[:R1, j * RB : (j + 1) * RB], u[R1:, j * RB : (j + 1) * RB], tr, ti), 1
                )
                for j in range(group)
            ],
            0,
        )
        s = dot(u, mats[1])
        tr, ti = slots[0], slots[1]
        s = jnp.concatenate(
            [
                jnp.concatenate(
                    times(s[j * R1 : (j + 1) * R1, :RB], s[j * R1 : (j + 1) * R1, RB:], tr, ti), 1
                )
                for j in range(group)
            ],
            0,
        )
        v = dot(s, mats[2])
        tr, ti = tables[2], tables[3]
        v = jnp.concatenate(
            [
                jnp.concatenate(
                    times(v[j * R1 : (j + 1) * R1, :RB], v[j * R1 : (j + 1) * R1, RB:], tr, ti), 0
                )
                for j in range(group)
            ],
            1,
        )
        r = dot(mats[3], v)
        for j in range(group):
            for part in range(2):
                cells[part, pl.ds(g * group + j, R1, stride=pulses), :] = r[
                    part * R1 : (part + 1) * R1, j * RB : (j + 1) * RB
                ]
        return carry

    lax.fori_loop(0, pulses // group, step, 0)

    lane = lax.broadcasted_iota(jnp.int32, (pulses, RB), 1)
    mine = (lane < RB // 4) | (lane >= RB - RB // 4)
    zero = jnp.zeros((pulses, RB), F32)

    for d in range(ranks):
        packed = []
        for part in range(2):
            after = zero if d == ranks - 1 else cells[part, pl.ds((d + 1) * blocks * pulses, pulses), :]
            before = zero if d == 0 else cells[part, pl.ds((d * blocks - 1) * pulses, pulses), :]
            packed.append(jnp.where(lane < RB // 2, after, before))
        send_ref[d, :pulses, :] = jnp.where(
            mine, packed[0], pltpu.roll(packed[1], RB // 2, 1)
        ).astype(BF16)
        for b in range(blocks):
            for part in range(2):
                begin = pulses + (2 * b + part) * pulses
                send_ref[d, begin : begin + pulses, :] = cells[
                    part, pl.ds((d * blocks + b) * pulses, pulses), :
                ].astype(BF16)


def turn_kernel(
    ranks, chunk, send_hbm, kernels_hbm, shift_hbm, phase_hbm, az_hbm, ahead_hbm, centroid_ref,
    out_ref, got, doppler, weights, filters, moves,
    kernels_ref, shift_ref, phase_ref, az_ref, ahead, sems, send_sems, got_sems,
):
    me = lax.axis_index("range")
    blocks, total = shift_ref.shape
    pulses = total // ranks
    taps, phases = kernels_ref.shape
    lead = taps // 2 - 1
    chunks = blocks // chunk

    barrier = pltpu.get_barrier_semaphore()

    def greet(k, carry):
        pl.semaphore_signal(
            barrier, inc=1, device_id={"range": lax.rem(me + k, ranks)},
            device_id_type=pl.DeviceIdType.MESH,
        )
        return carry

    lax.fori_loop(1, ranks, greet, 0)
    copies = fetch(
        [
            (kernels_hbm, kernels_ref), (shift_hbm, shift_ref), (phase_hbm, phase_ref),
            (az_hbm, az_ref), (ahead_hbm, ahead), (send_hbm.at[me], got.at[me]),
        ],
        sems,
    )
    pl.semaphore_wait(barrier, ranks - 1)

    def rows(c):
        if c == 0:
            return pl.ds(0, pulses + 2 * chunk * pulses)
        return pl.ds(pulses + 2 * c * chunk * pulses, 2 * chunk * pulses)

    def remote(c, to, owner):
        return pltpu.make_async_remote_copy(
            src_ref=send_hbm.at[to, rows(c)],
            dst_ref=got.at[owner, rows(c)],
            send_sem=send_sems.at[c, to],
            recv_sem=got_sems.at[c, owner],
            device_id={"range": to},
            device_id_type=pl.DeviceIdType.MESH,
        )

    half = ranks // 2
    for c in range(chunks):

        def begin(k, carry):
            remote(c, lax.rem(me + k, ranks), me).start()
            return carry

        lax.fori_loop(half, ranks, begin, 0)
        lax.fori_loop(1, half, begin, 0)

    for copy in copies:
        copy.wait()

    wide = lax.broadcasted_iota(jnp.int32, (blocks, 1), 0)
    turns = jnp.zeros((blocks, 1), jnp.int32)
    for b in range(blocks):
        turns = jnp.where(wide == b, centroid_ref[b], turns)
    turns = jnp.broadcast_to(turns, (blocks, total))
    lines = []
    for part in range(2):
        line = az_ref[part]
        step = 1
        while step < total:
            line = jnp.where((turns & step) != 0, pltpu.roll(line, step, 1), line)
            step *= 2
        lines.append(line)
    lines.append(shift_ref[...].astype(F32))
    lines.append(phase_ref[...].astype(F32))
    lines.append(jnp.zeros((RB - 4 * blocks, total), F32))
    columns = jnp.concatenate(lines, 0).T

    def column(j):
        return jnp.broadcast_to(columns[:, j : j + 1], (total, RB))

    left = jnp.concatenate([kernels_ref[...], jnp.zeros((taps, RB - phases), F32)], 1).T
    terms = []
    for _ in range(3):
        term = left.astype(BF16)
        left = left - term.astype(F32)
        terms.append(term[:phases])
    terms.append(jnp.zeros((RB - 3 * phases, taps), BF16))
    table = jnp.concatenate(terms, 0).astype(F32)
    table = jnp.concatenate(
        [jnp.broadcast_to(table[:, t : t + 1], (RB, RB)) for t in range(taps)], 1
    ).astype(BF16)
    slot = lax.broadcasted_iota(jnp.int32, (total, RB), 1)
    slot = jnp.where(slot < 3 * phases, lax.rem(slot, phases), -1)

    for b in range(blocks):
        filters[b, 0] = column(b)
        filters[b, 1] = column(blocks + b)
        moves[b] = column(2 * blocks + b).astype(jnp.int32)
        chosen = jnp.where(column(3 * blocks + b).astype(jnp.int32) == slot, 1.0, 0.0).astype(BF16)
        for t in range(0, taps, 2):
            pair_of = dot(chosen, table[:, t * RB : (t + 2) * RB])
            weights[b, t] = pair_of[:, :RB]
            weights[b, t + 1] = pair_of[:, RB:]

    size = 32
    lane = lax.broadcasted_iota(jnp.int32, (size, RB), 1)

    def focus(b):
        for row in range(0, total, size):
            here = pl.ds(row, size)
            shift = moves[b, here, :]
            where = (lane + shift + (RB - lead)) & (RB - 1)
            early = lane < RB - shift
            found = []
            for part in range(2):
                at = pl.ds(part * total + row, size)
                prev, cur, after = doppler[b, at, :], doppler[b + 1, at, :], doppler[b + 2, at, :]
                a = jnp.take_along_axis(jnp.where(lane >= RB - lead, prev, cur), where, axis=1)
                z = jnp.take_along_axis(jnp.where(lane >= RB - lead, cur, after), where, axis=1)
                x = jnp.where(early, a, z)
                summed = weights[b, 0, here, :] * x
                for t in range(1, taps):
                    summed += weights[b, t, here, :] * pltpu.roll(jnp.where(lane < t, z, x), RB - t, 1)
                found.append(summed)
            ar, ai = filters[b, 0, here, :], filters[b, 1, here, :]
            cells = pl.ds(b * RB, RB)
            out_ref[here, cells] = (found[0] * ar - found[1] * ai).astype(BF16)
            out_ref[pl.ds(total + row, size), cells] = (found[0] * ai + found[1] * ar).astype(BF16)

    for c in range(chunks):

        def arrive(k, carry):
            remote(c, me, lax.rem(me + k, ranks)).wait_recv()
            return carry

        lax.fori_loop(1, ranks, arrive, 0)
        if c == 0:
            halo = got[:, :pulses, :]
            turned = jnp.concatenate([halo[:, :, RB // 2 :], halo[:, :, : RB // 2]], 2)
            edge = jnp.stack([halo, turned], 1).reshape(2 * total, RB)
            edge = dot(ahead[...], edge)
            doppler[0] = edge
            doppler[blocks + 1] = edge
        for b in range(c * chunk, (c + 1) * chunk):
            begin_row = pulses + 2 * b * pulses
            x = got[:, begin_row : begin_row + 2 * pulses, :].reshape(2 * total, RB)
            doppler[b + 1] = dot(ahead[...], x)
        for b in range(max(c * chunk - 1, 0), (c + 1) * chunk - (c < chunks - 1)):
            focus(b)

    for c in range(chunks):

        def leave(k, carry):
            remote(c, lax.rem(me + k, ranks), me).wait_send()
            return carry

        lax.fori_loop(1, ranks, leave, 0)


def local(echoes, range_reference, kernels, shifts, phase_index, centroid, azimuth_reference):
    ranks = lax.axis_size("range")
    pulses, samples = echoes.shape[1:]
    second = samples // R1
    blocks = R1 // ranks
    total = ranks * pulses
    taps = kernels.shape[1]
    mats = np.stack([
        left_matrix(roots(R1, -1.0)),
        right_matrix(roots(second, -1.0)),
        right_matrix(roots(second, 1.0)),
        left_matrix(roots(R1, 1.0)),
    ])
    tables = np.concatenate([
        pair(twist(R1, second, -1.0) / math.sqrt(samples)),
        pair(twist(R1, second, 1.0) / math.sqrt(samples)),
    ])
    turn = azimuth_matrix(ranks, pulses)
    ahead = left_matrix(turn).reshape(2 * total, 2, ranks, pulses).transpose(0, 2, 1, 3)
    ahead = ahead.reshape(2 * total, 2 * total)
    back = left_matrix(turn.conj().T)
    vmem = pl.BlockSpec(memory_space=pltpu.VMEM)
    anywhere = pl.BlockSpec(memory_space=pl.ANY)
    height = 2 * blocks * pulses + pulses
    dma = pltpu.SemaphoreType.DMA
    send = pl.pallas_call(
        functools.partial(range_kernel, ranks, math.gcd(pulses, 4)),
        out_shape=jax.ShapeDtypeStruct((ranks, height, RB), BF16),
        in_specs=[anywhere] * 4,
        out_specs=vmem,
        scratch_shapes=[
            pltpu.VMEM((2, R1 * pulses, RB), F32),
            pltpu.VMEM((2, R1 * pulses, RB), F32),
            pltpu.VMEM((2, R1, second), F32),
            pltpu.VMEM(echoes.shape, BF16),
            pltpu.VMEM(range_reference.shape, F32),
            pltpu.VMEM(mats.shape, BF16),
            pltpu.VMEM(tables.shape, F32),
            dma((4,)),
        ],
        compiler_params=pltpu.CompilerParams(vmem_limit_bytes=VMEM_BYTES),
        name="range_lines",
    )(echoes, range_reference, mats, tables)
    chunk = max(1, blocks // 4)
    focused = pl.pallas_call(
        functools.partial(turn_kernel, ranks, chunk),
        out_shape=jax.ShapeDtypeStruct((2 * total, blocks * RB), BF16),
        in_specs=[anywhere] * 6 + [pl.BlockSpec(memory_space=pltpu.SMEM)],
        out_specs=vmem,
        scratch_shapes=[
            pltpu.VMEM((ranks, height, RB), BF16),
            pltpu.VMEM((blocks + 2, 2 * total, RB), F32),
            pltpu.VMEM((blocks, taps, total, RB), F32),
            pltpu.VMEM((blocks, 2, total, RB), F32),
            pltpu.VMEM((blocks, total, RB), jnp.int32),
            pltpu.VMEM(kernels.shape[::-1], F32),
            pltpu.VMEM(shifts.shape, jnp.int32),
            pltpu.VMEM(shifts.shape, jnp.int32),
            pltpu.VMEM(azimuth_reference.shape, F32),
            pltpu.VMEM(ahead.shape, BF16),
            dma((6,)),
            dma((blocks // chunk, ranks)),
            dma((blocks // chunk, ranks)),
        ],
        compiler_params=pltpu.CompilerParams(
            vmem_limit_bytes=VMEM_BYTES, collective_id=0, has_side_effects=True
        ),
        name="turn_and_azimuth",
    )(send, kernels.T, shifts, phase_index, azimuth_reference, ahead, centroid)
    return dot(back, focused).astype(BF16).reshape(2, total, blocks * RB)


def solution(mesh):
    in_specs = (
        P("groups", "range", None),
        P(),
        P(),
        P("range", None),
        P("range", None),
        P("range"),
        P(None, "range", None),
    )
    out_specs = P("groups", None, "range")
    return jax.shard_map(local, mesh=mesh, in_specs=in_specs, out_specs=out_specs, check_vma=False)
```

```python
import functools
import math

import jax
import jax.numpy as jnp
import ml_dtypes
import numpy as np
from jax import lax
from jax.experimental import pallas as pl
from jax.experimental.pallas import tpu as pltpu
from jax.sharding import PartitionSpec as P

R1 = 128
RB = 128
F32 = jnp.float32
BF16 = jnp.bfloat16
VMEM_BYTES = 58 << 20


def roots(length, orient):
    line = np.arange(length)
    angles = 2.0 * math.pi / length * (line[:, None] * line[None, :] % length)
    rounded = lambda part: part.astype(ml_dtypes.bfloat16).astype(np.float64)
    return rounded(np.cos(angles)) + 1j * orient * rounded(np.sin(angles))


def twist(first_len, second_len, orient):
    whole = first_len * second_len
    turns = np.arange(first_len)[:, None] * np.arange(second_len)[None, :] % whole
    return np.exp(orient * 2j * math.pi / whole * turns)


def left_matrix(m):
    return np.block([[m.real, -m.imag], [m.imag, m.real]]).astype(ml_dtypes.bfloat16)


def right_matrix(m):
    return np.block([[m.real, m.imag], [-m.imag, m.real]]).astype(ml_dtypes.bfloat16)


def pair(m):
    return np.stack([m.real, m.imag]).astype(np.float32)


def azimuth_matrix(first, second):
    parts = np.einsum(
        "ka,mk,bm->bkam", roots(first, -1.0), twist(second, first, -1.0), roots(second, -1.0)
    )
    return parts.reshape(first * second, first * second) / math.sqrt(first * second)


def dot(a, b):
    return jnp.dot(a, b, preferred_element_type=F32)


def fetch(pairs, sems):
    copies = [pltpu.make_async_copy(src, dst, sems.at[i]) for i, (src, dst) in enumerate(pairs)]
    for copy in copies:
        copy.start()
    return copies


def range_kernel(
    ranks, group, e_hbm, ref_hbm, mats_hbm, tables_hbm, send_ref,
    lines, cells, slots, e_ref, ref_ref, mats, tables, sems,
):
    pulses = e_ref.shape[1]
    blocks = R1 // ranks
    copies = fetch(
        [(e_hbm, e_ref), (ref_hbm, ref_ref), (tables_hbm, tables), (mats_hbm, mats)], sems
    )
    copies[0].wait()

    def spread(n1, carry):
        lane = pl.multiple_of(n1 * RB, RB)
        for part in range(2):
            lines[part, pl.ds(n1, pulses, stride=R1), :] = e_ref[part, :, pl.ds(lane, RB)].astype(F32)
        return carry

    lax.fori_loop(0, R1, spread, 0, unroll=32)
    for copy in copies[1:]:
        copy.wait()
    for part in range(2):
        for k2 in range(ref_ref.shape[1] // R1):
            slots[part, k2 : k2 + 1, :] = ref_ref[part : part + 1, k2 * R1 : (k2 + 1) * R1]
    for part in range(2):
        slots[part] = slots[part].T

    def times(re, im, tr, ti):
        return (re * tr - im * ti).astype(BF16), (re * ti + im * tr).astype(BF16)

    def step(g, carry):
        def line(part, j):
            return lines[part, pl.ds((g * group + j) * R1, R1), :].astype(BF16)

        x = jnp.concatenate(
            [jnp.concatenate([line(part, j) for j in range(group)], 1) for part in range(2)], 0
        )
        u = dot(mats[0], x)
        tr, ti = tables[0], tables[1]
        u = jnp.concatenate(
            [
                jnp.concatenate(
                    times(u[:R1, j * RB : (j + 1) * RB], u[R1:, j * RB : (j + 1) * RB], tr, ti), 1
                )
                for j in range(group)
            ],
            0,
        )
        s = dot(u, mats[1])
        tr, ti = slots[0], slots[1]
        s = jnp.concatenate(
            [
                jnp.concatenate(
                    times(s[j * R1 : (j + 1) * R1, :RB], s[j * R1 : (j + 1) * R1, RB:], tr, ti), 1
                )
                for j in range(group)
            ],
            0,
        )
        v = dot(s, mats[2])
        tr, ti = tables[2], tables[3]
        v = jnp.concatenate(
            [
                jnp.concatenate(
                    times(v[j * R1 : (j + 1) * R1, :RB], v[j * R1 : (j + 1) * R1, RB:], tr, ti), 0
                )
                for j in range(group)
            ],
            1,
        )
        r = dot(mats[3], v)
        for j in range(group):
            for part in range(2):
                cells[part, pl.ds(g * group + j, R1, stride=pulses), :] = r[
                    part * R1 : (part + 1) * R1, j * RB : (j + 1) * RB
                ]
        return carry

    for g in range(pulses // group):
        step(g, 0)

    lane = lax.broadcasted_iota(jnp.int32, (pulses, RB), 1)
    mine = (lane < RB // 4) | (lane >= RB - RB // 4)
    zero = jnp.zeros((pulses, RB), F32)

    for d in range(ranks):
        packed = []
        for part in range(2):
            after = zero if d == ranks - 1 else cells[part, pl.ds((d + 1) * blocks * pulses, pulses), :]
            before = zero if d == 0 else cells[part, pl.ds((d * blocks - 1) * pulses, pulses), :]
            packed.append(jnp.where(lane < RB // 2, after, before))
        send_ref[d, :pulses, :] = jnp.where(
            mine, packed[0], pltpu.roll(packed[1], RB // 2, 1)
        ).astype(BF16)
        for b in range(blocks):
            for part in range(2):
                begin = pulses + (2 * b + part) * pulses
                send_ref[d, begin : begin + pulses, :] = cells[
                    part, pl.ds((d * blocks + b) * pulses, pulses), :
                ].astype(BF16)


def turn_kernel(
    ranks, chunk, send_hbm, kernels_hbm, shift_hbm, phase_hbm, az_hbm, ahead_hbm, centroid_ref,
    out_ref, got, doppler, weights, filters, moves,
    kernels_ref, shift_ref, phase_ref, az_ref, ahead, sems, send_sems, got_sems,
):
    me = lax.axis_index("range")
    blocks, total = shift_ref.shape
    pulses = total // ranks
    taps, phases = kernels_ref.shape
    lead = taps // 2 - 1
    chunks = blocks // chunk

    barrier = pltpu.get_barrier_semaphore()

    def greet(k, carry):
        pl.semaphore_signal(
            barrier, inc=1, device_id={"range": lax.rem(me + k, ranks)},
            device_id_type=pl.DeviceIdType.MESH,
        )
        return carry

    lax.fori_loop(1, ranks, greet, 0)
    copies = fetch(
        [
            (kernels_hbm, kernels_ref), (shift_hbm, shift_ref), (phase_hbm, phase_ref),
            (az_hbm, az_ref), (ahead_hbm, ahead), (send_hbm.at[me], got.at[me]),
        ],
        sems,
    )
    pl.semaphore_wait(barrier, ranks - 1)

    def rows(c):
        if c == 0:
            return pl.ds(0, pulses + 2 * chunk * pulses)
        return pl.ds(pulses + 2 * c * chunk * pulses, 2 * chunk * pulses)

    def remote(c, to, owner):
        return pltpu.make_async_remote_copy(
            src_ref=send_hbm.at[to, rows(c)],
            dst_ref=got.at[owner, rows(c)],
            send_sem=send_sems.at[c, to],
            recv_sem=got_sems.at[c, owner],
            device_id={"range": to},
            device_id_type=pl.DeviceIdType.MESH,
        )

    half = ranks // 2

    def depart(c):
        def begin(k, carry):
            remote(c, lax.rem(me + k, ranks), me).start()
            return carry

        lax.fori_loop(half, ranks, begin, 0)
        lax.fori_loop(1, half, begin, 0)

    for c in range(min(2, chunks)):
        depart(c)

    for copy in copies:
        copy.wait()

    wide = lax.broadcasted_iota(jnp.int32, (blocks, 1), 0)
    turns = jnp.zeros((blocks, 1), jnp.int32)
    for b in range(blocks):
        turns = jnp.where(wide == b, centroid_ref[b], turns)
    turns = jnp.broadcast_to(turns, (blocks, total))
    lines = []
    for part in range(2):
        line = az_ref[part]
        step = 1
        while step < total:
            line = jnp.where((turns & step) != 0, pltpu.roll(line, step, 1), line)
            step *= 2
        lines.append(line)
    lines.append(shift_ref[...].astype(F32))
    lines.append(phase_ref[...].astype(F32))
    lines.append(jnp.zeros((RB - 4 * blocks, total), F32))
    columns = jnp.concatenate(lines, 0).T

    def column(j):
        return jnp.broadcast_to(columns[:, j : j + 1], (total, RB))

    left = jnp.concatenate([kernels_ref[...], jnp.zeros((taps, RB - phases), F32)], 1).T
    terms = []
    for _ in range(3):
        term = left.astype(BF16)
        left = left - term.astype(F32)
        terms.append(term[:phases])
    terms.append(jnp.zeros((RB - 3 * phases, taps), BF16))
    table = jnp.concatenate(terms, 0).astype(F32)
    table = jnp.concatenate(
        [jnp.broadcast_to(table[:, t : t + 1], (RB, RB)) for t in range(taps)], 1
    ).astype(BF16)
    slot = lax.broadcasted_iota(jnp.int32, (total, RB), 1)
    slot = jnp.where(slot < 3 * phases, lax.rem(slot, phases), -1)

    for b in range(blocks):
        filters[b, 0] = column(b)
        filters[b, 1] = column(blocks + b)
        moves[b] = column(2 * blocks + b).astype(jnp.int32)
        chosen = jnp.where(column(3 * blocks + b).astype(jnp.int32) == slot, 1.0, 0.0).astype(BF16)
        for t in range(0, taps, 2):
            pair_of = dot(chosen, table[:, t * RB : (t + 2) * RB])
            weights[b, t] = pair_of[:, :RB]
            weights[b, t + 1] = pair_of[:, RB:]

    size = 32
    lane = lax.broadcasted_iota(jnp.int32, (size, RB), 1)

    def focus(b):
        for row in range(0, total, size):
            here = pl.ds(row, size)
            shift = moves[b, here, :]
            where = (lane + shift + (RB - lead)) & (RB - 1)
            early = lane < RB - shift
            found = []
            for part in range(2):
                at = pl.ds(part * total + row, size)
                prev, cur, after = doppler[b, at, :], doppler[b + 1, at, :], doppler[b + 2, at, :]
                a = jnp.take_along_axis(jnp.where(lane >= RB - lead, prev, cur), where, axis=1)
                z = jnp.take_along_axis(jnp.where(lane >= RB - lead, cur, after), where, axis=1)
                x = jnp.where(early, a, z)
                summed = weights[b, 0, here, :] * x
                for t in range(1, taps):
                    summed += weights[b, t, here, :] * pltpu.roll(jnp.where(lane < t, z, x), RB - t, 1)
                found.append(summed)
            ar, ai = filters[b, 0, here, :], filters[b, 1, here, :]
            cells = pl.ds(b * RB, RB)
            out_ref[here, cells] = (found[0] * ar - found[1] * ai).astype(BF16)
            out_ref[pl.ds(total + row, size), cells] = (found[0] * ai + found[1] * ar).astype(BF16)

    for c in range(chunks):

        def arrive(k, carry):
            remote(c, me, lax.rem(me + k, ranks)).wait_recv()
            return carry

        lax.fori_loop(1, ranks, arrive, 0)
        if c + 2 < chunks:
            depart(c + 2)
        if c == 0:
            halo = got[:, :pulses, :]
            turned = jnp.concatenate([halo[:, :, RB // 2 :], halo[:, :, : RB // 2]], 2)
            edge = jnp.stack([halo, turned], 1).reshape(2 * total, RB)
            edge = dot(ahead[...], edge)
            doppler[0] = edge
            doppler[blocks + 1] = edge
        for b in range(c * chunk, (c + 1) * chunk):
            begin_row = pulses + 2 * b * pulses
            x = got[:, begin_row : begin_row + 2 * pulses, :].reshape(2 * total, RB)
            doppler[b + 1] = dot(ahead[...], x)
        for b in range(max(c * chunk - 1, 0), (c + 1) * chunk - (c < chunks - 1)):
            focus(b)

    for c in range(chunks):

        def leave(k, carry):
            remote(c, lax.rem(me + k, ranks), me).wait_send()
            return carry

        lax.fori_loop(1, ranks, leave, 0)


def local(echoes, range_reference, kernels, shifts, phase_index, centroid, azimuth_reference):
    ranks = lax.axis_size("range")
    pulses, samples = echoes.shape[1:]
    second = samples // R1
    blocks = R1 // ranks
    total = ranks * pulses
    taps = kernels.shape[1]
    mats = np.stack([
        left_matrix(roots(R1, -1.0)),
        right_matrix(roots(second, -1.0)),
        right_matrix(roots(second, 1.0)),
        left_matrix(roots(R1, 1.0)),
    ])
    tables = np.concatenate([
        pair(twist(R1, second, -1.0) / math.sqrt(samples)),
        pair(twist(R1, second, 1.0) / math.sqrt(samples)),
    ])
    turn = azimuth_matrix(ranks, pulses)
    ahead = left_matrix(turn).reshape(2 * total, 2, ranks, pulses).transpose(0, 2, 1, 3)
    ahead = ahead.reshape(2 * total, 2 * total)
    back = left_matrix(turn.conj().T)
    vmem = pl.BlockSpec(memory_space=pltpu.VMEM)
    anywhere = pl.BlockSpec(memory_space=pl.ANY)
    height = 2 * blocks * pulses + pulses
    dma = pltpu.SemaphoreType.DMA
    send = pl.pallas_call(
        functools.partial(range_kernel, ranks, math.gcd(pulses, 4)),
        out_shape=jax.ShapeDtypeStruct((ranks, height, RB), BF16),
        in_specs=[anywhere] * 4,
        out_specs=vmem,
        scratch_shapes=[
            pltpu.VMEM((2, R1 * pulses, RB), F32),
            pltpu.VMEM((2, R1 * pulses, RB), F32),
            pltpu.VMEM((2, R1, second), F32),
            pltpu.VMEM(echoes.shape, BF16),
            pltpu.VMEM(range_reference.shape, F32),
            pltpu.VMEM(mats.shape, BF16),
            pltpu.VMEM(tables.shape, F32),
            dma((4,)),
        ],
        compiler_params=pltpu.CompilerParams(vmem_limit_bytes=VMEM_BYTES),
        name="range_lines",
    )(echoes, range_reference, mats, tables)
    chunk = max(1, blocks // 4)
    focused = pl.pallas_call(
        functools.partial(turn_kernel, ranks, chunk),
        out_shape=jax.ShapeDtypeStruct((2 * total, blocks * RB), BF16),
        in_specs=[anywhere] * 6 + [pl.BlockSpec(memory_space=pltpu.SMEM)],
        out_specs=vmem,
        scratch_shapes=[
            pltpu.VMEM((ranks, height, RB), BF16),
            pltpu.VMEM((blocks + 2, 2 * total, RB), F32),
            pltpu.VMEM((blocks, taps, total, RB), F32),
            pltpu.VMEM((blocks, 2, total, RB), F32),
            pltpu.VMEM((blocks, total, RB), jnp.int32),
            pltpu.VMEM(kernels.shape[::-1], F32),
            pltpu.VMEM(shifts.shape, jnp.int32),
            pltpu.VMEM(shifts.shape, jnp.int32),
            pltpu.VMEM(azimuth_reference.shape, F32),
            pltpu.VMEM(ahead.shape, BF16),
            dma((6,)),
            dma((blocks // chunk, ranks)),
            dma((blocks // chunk, ranks)),
        ],
        compiler_params=pltpu.CompilerParams(
            vmem_limit_bytes=VMEM_BYTES, collective_id=0, has_side_effects=True
        ),
        name="turn_and_azimuth",
    )(send, kernels.T, shifts, phase_index, azimuth_reference, ahead, centroid)
    return dot(back, focused).astype(BF16).reshape(2, total, blocks * RB)


def solution(mesh):
    in_specs = (
        P("groups", "range", None),
        P(),
        P(),
        P("range", None),
        P("range", None),
        P("range"),
        P(None, "range", None),
    )
    out_specs = P("groups", None, "range")
    return jax.shard_map(local, mesh=mesh, in_specs=in_specs, out_specs=out_specs, check_vma=False)
```

```python
import functools
import math

import jax
import jax.numpy as jnp
import ml_dtypes
import numpy as np
from jax import lax
from jax.experimental import pallas as pl
from jax.experimental.pallas import tpu as pltpu
from jax.sharding import PartitionSpec as P

R1 = 128
RB = 128
F32 = jnp.float32
BF16 = jnp.bfloat16
VMEM_BYTES = 58 << 20


def roots(length, orient):
    line = np.arange(length)
    angles = 2.0 * math.pi / length * (line[:, None] * line[None, :] % length)
    rounded = lambda part: part.astype(ml_dtypes.bfloat16).astype(np.float64)
    return rounded(np.cos(angles)) + 1j * orient * rounded(np.sin(angles))


def twist(first_len, second_len, orient):
    whole = first_len * second_len
    turns = np.arange(first_len)[:, None] * np.arange(second_len)[None, :] % whole
    return np.exp(orient * 2j * math.pi / whole * turns)


def left_matrix(m):
    return np.block([[m.real, -m.imag], [m.imag, m.real]]).astype(ml_dtypes.bfloat16)


def right_matrix(m):
    return np.block([[m.real, m.imag], [-m.imag, m.real]]).astype(ml_dtypes.bfloat16)


def pair(m):
    return np.stack([m.real, m.imag]).astype(np.float32)


def azimuth_matrix(first, second):
    parts = np.einsum(
        "ka,mk,bm->bkam", roots(first, -1.0), twist(second, first, -1.0), roots(second, -1.0)
    )
    return parts.reshape(first * second, first * second) / math.sqrt(first * second)


def dot(a, b):
    return jnp.dot(a, b, preferred_element_type=F32)


def fetch(pairs, sems):
    copies = [pltpu.make_async_copy(src, dst, sems.at[i]) for i, (src, dst) in enumerate(pairs)]
    for copy in copies:
        copy.start()
    return copies


def turn_kernel(
    ranks, group, chunk, e_hbm, ref_hbm, tables_hbm, mats_hbm,
    kernels_hbm, shift_hbm, phase_hbm, az_hbm, ahead_hbm, centroid_ref,
    out_ref, lines, cells, slots, early_send, late_send, early_got, late_got,
    doppler, weights, filters, moves, e_ref, ref_ref, tables, mats,
    kernels_ref, shift_ref, phase_ref, az_ref, ahead, sems, send_sems, got_sems,
):
    me = lax.axis_index("range")
    blocks, total = shift_ref.shape
    pulses = total // ranks
    taps, phases = kernels_ref.shape
    lead = taps // 2 - 1
    chunks = blocks // chunk

    barrier = pltpu.get_barrier_semaphore()

    def greet(k, carry):
        pl.semaphore_signal(
            barrier, inc=1, device_id={"range": lax.rem(me + k, ranks)},
            device_id_type=pl.DeviceIdType.MESH,
        )
        return carry

    lax.fori_loop(1, ranks, greet, 0)
    copies = fetch(
        [
            (e_hbm, e_ref), (ref_hbm, ref_ref), (tables_hbm, tables), (mats_hbm, mats),
            (kernels_hbm, kernels_ref), (shift_hbm, shift_ref), (phase_hbm, phase_ref),
            (az_hbm, az_ref), (ahead_hbm, ahead),
        ],
        sems,
    )
    copies[0].wait()
    part_pulses = pulses // 2

    def spread(n1, carry):
        lane = pl.multiple_of(n1 * RB, RB)
        for part in range(2):
            lines[part, pl.ds(n1, pulses, stride=R1), :] = e_ref[part, :, pl.ds(lane, RB)].astype(F32)
        return carry

    lax.fori_loop(0, R1, spread, 0, unroll=32)
    for copy in copies[1:4]:
        copy.wait()
    for part in range(2):
        for k2 in range(ref_ref.shape[1] // R1):
            slots[part, k2 : k2 + 1, :] = ref_ref[part : part + 1, k2 * R1 : (k2 + 1) * R1]
    for part in range(2):
        slots[part] = slots[part].T

    def times(re, im, tr, ti):
        return (re * tr - im * ti).astype(BF16), (re * ti + im * tr).astype(BF16)

    def step(g, carry):
        def line(part, j):
            return lines[part, pl.ds((g * group + j) * R1, R1), :].astype(BF16)

        x = jnp.concatenate(
            [jnp.concatenate([line(part, j) for j in range(group)], 1) for part in range(2)], 0
        )
        u = dot(mats[0], x)
        tr, ti = tables[0], tables[1]
        u = jnp.concatenate(
            [
                jnp.concatenate(
                    times(u[:R1, j * RB : (j + 1) * RB], u[R1:, j * RB : (j + 1) * RB], tr, ti), 1
                )
                for j in range(group)
            ],
            0,
        )
        s = dot(u, mats[1])
        tr, ti = slots[0], slots[1]
        s = jnp.concatenate(
            [
                jnp.concatenate(
                    times(s[j * R1 : (j + 1) * R1, :RB], s[j * R1 : (j + 1) * R1, RB:], tr, ti), 1
                )
                for j in range(group)
            ],
            0,
        )
        v = dot(s, mats[2])
        tr, ti = tables[2], tables[3]
        v = jnp.concatenate(
            [
                jnp.concatenate(
                    times(v[j * R1 : (j + 1) * R1, :RB], v[j * R1 : (j + 1) * R1, RB:], tr, ti), 0
                )
                for j in range(group)
            ],
            1,
        )
        r = dot(mats[3], v)
        for j in range(group):
            for part in range(2):
                cells[part, pl.ds(g * group + j, R1, stride=pulses), :] = r[
                    part * R1 : (part + 1) * R1, j * RB : (j + 1) * RB
                ]
        return carry

    def transform(h):
        steps = part_pulses // group
        for g in range(h * steps, (h + 1) * steps):
            step(g, 0)

    def pack(h, d, b):
        begin = (d * blocks + b) * pulses + h * part_pulses
        return jnp.concatenate(
            [cells[part, pl.ds(begin, part_pulses), :] for part in range(2)], 0
        ).astype(BF16)

    def rows(c):
        if c == 1:
            return pl.ds(0, pulses + chunk * pulses)
        return pl.ds(pulses + (c - 1) * chunk * pulses, chunk * pulses)

    def remote(c, to, owner):
        if c == 0:
            src, dst = early_send.at[to], early_got.at[owner]
        else:
            src, dst = late_send.at[to, rows(c)], late_got.at[owner, rows(c)]
        return pltpu.make_async_remote_copy(
            src_ref=src,
            dst_ref=dst,
            send_sem=send_sems.at[c, to],
            recv_sem=got_sems.at[c, owner],
            device_id={"range": to},
            device_id_type=pl.DeviceIdType.MESH,
        )

    half = ranks // 2
    side = me // half

    def depart(c):
        def across(k, carry):
            remote(c, (1 - side) * half + lax.rem(me + k, half), me).start()
            return carry

        def near(k, carry):
            remote(c, side * half + lax.rem(me + k, half), me).start()
            return carry

        lax.fori_loop(0, half, across, 0)
        lax.fori_loop(1, half, near, 0)

    transform(0)
    for d in range(ranks):
        for b in range(blocks):
            early_send[d, b * pulses : (b + 1) * pulses, :] = pack(0, d, b)
    pl.semaphore_wait(barrier, ranks - 1)
    depart(0)
    own_early = pltpu.make_async_copy(early_send.at[me], early_got.at[me], sems.at[9])
    own_early.start()
    transform(1)
    spot = lax.broadcasted_iota(jnp.int32, (pulses, RB), 1)
    mine = (spot < RB // 4) | (spot >= RB - RB // 4)
    zero = jnp.zeros((pulses, RB), F32)
    for d in range(ranks):
        packed = []
        for part in range(2):
            after = zero if d == ranks - 1 else cells[part, pl.ds((d + 1) * blocks * pulses, pulses), :]
            before = zero if d == 0 else cells[part, pl.ds((d * blocks - 1) * pulses, pulses), :]
            packed.append(jnp.where(spot < RB // 2, after, before))
        late_send[d, :pulses, :] = jnp.where(
            mine, packed[0], pltpu.roll(packed[1], RB // 2, 1)
        ).astype(BF16)
        for b in range(blocks):
            late_send[d, (b + 1) * pulses : (b + 2) * pulses, :] = pack(1, d, b)
    own_late = pltpu.make_async_copy(late_send.at[me], late_got.at[me], sems.at[10])
    own_late.start()
    for c in range(1, min(2, chunks) + 1):
        depart(c)
    for copy in copies[4:]:
        copy.wait()

    wide = lax.broadcasted_iota(jnp.int32, (blocks, 1), 0)
    turns = jnp.zeros((blocks, 1), jnp.int32)
    for b in range(blocks):
        turns = jnp.where(wide == b, centroid_ref[b], turns)
    turns = jnp.broadcast_to(turns, (blocks, total))
    lines = []
    for part in range(2):
        line = az_ref[part]
        step = 1
        while step < total:
            line = jnp.where((turns & step) != 0, pltpu.roll(line, step, 1), line)
            step *= 2
        lines.append(line)
    lines.append(shift_ref[...].astype(F32))
    lines.append(phase_ref[...].astype(F32))
    lines.append(jnp.zeros((RB - 4 * blocks, total), F32))
    columns = jnp.concatenate(lines, 0).T

    def column(j):
        return jnp.broadcast_to(columns[:, j : j + 1], (total, RB))

    left = jnp.concatenate([kernels_ref[...], jnp.zeros((taps, RB - phases), F32)], 1).T
    terms = []
    for _ in range(3):
        term = left.astype(BF16)
        left = left - term.astype(F32)
        terms.append(term[:phases])
    terms.append(jnp.zeros((RB - 3 * phases, taps), BF16))
    table = jnp.concatenate(terms, 0).astype(F32)
    table = jnp.concatenate(
        [jnp.broadcast_to(table[:, t : t + 1], (RB, RB)) for t in range(taps)], 1
    ).astype(BF16)
    slot = lax.broadcasted_iota(jnp.int32, (total, RB), 1)
    slot = jnp.where(slot < 3 * phases, lax.rem(slot, phases), -1)

    for b in range(blocks):
        filters[b, 0] = column(b)
        filters[b, 1] = column(blocks + b)
        moves[b] = column(2 * blocks + b).astype(jnp.int32)
        chosen = jnp.where(column(3 * blocks + b).astype(jnp.int32) == slot, 1.0, 0.0).astype(BF16)
        for t in range(0, taps, 2):
            pair_of = dot(chosen, table[:, t * RB : (t + 2) * RB])
            weights[b, t] = pair_of[:, :RB]
            weights[b, t + 1] = pair_of[:, RB:]

    size = 32
    lane = lax.broadcasted_iota(jnp.int32, (size, RB), 1)

    def focus(b):
        for row in range(0, total, size):
            here = pl.ds(row, size)
            shift = moves[b, here, :]
            where = (lane + shift + (RB - lead)) & (RB - 1)
            early = lane < RB - shift
            found = []
            for part in range(2):
                at = pl.ds(part * total + row, size)
                prev, cur, after = doppler[b, at, :], doppler[b + 1, at, :], doppler[b + 2, at, :]
                a = jnp.take_along_axis(jnp.where(lane >= RB - lead, prev, cur), where, axis=1)
                z = jnp.take_along_axis(jnp.where(lane >= RB - lead, cur, after), where, axis=1)
                x = jnp.where(early, a, z)
                summed = weights[b, 0, here, :] * x
                for t in range(1, taps):
                    summed += weights[b, t, here, :] * pltpu.roll(jnp.where(lane < t, z, x), RB - t, 1)
                found.append(summed)
            ar, ai = filters[b, 0, here, :], filters[b, 1, here, :]
            cells = pl.ds(b * RB, RB)
            out_ref[here, cells] = (found[0] * ar - found[1] * ai).astype(BF16)
            out_ref[pl.ds(total + row, size), cells] = (found[0] * ai + found[1] * ar).astype(BF16)

    def arrive(c):
        def one(k, carry):
            remote(c, me, lax.rem(me + k, ranks)).wait_recv()
            return carry

        lax.fori_loop(1, ranks, one, 0)

    own_early.wait()
    own_late.wait()
    arrive(0)
    for b in range(blocks):
        x = early_got[:, b * pulses : (b + 1) * pulses, :].reshape(total, RB)
        doppler[b + 1] = dot(ahead[0], x)
    for c in range(chunks):
        arrive(c + 1)
        if c + 2 < chunks:
            depart(c + 3)
        if c == 0:
            halo = late_got[:, :pulses, :].astype(F32)
            turned = jnp.concatenate([halo[:, :, RB // 2 :], halo[:, :, : RB // 2]], 2)
            edge = jnp.zeros((2 * total, RB), F32)
            for h in range(2):
                at = slice(h * part_pulses, (h + 1) * part_pulses)
                x = jnp.concatenate([halo[:, at], turned[:, at]], 1).astype(BF16)
                edge += dot(ahead[h], x.reshape(total, RB))
            doppler[0] = edge
            doppler[blocks + 1] = edge
        for b in range(c * chunk, (c + 1) * chunk):
            x = late_got[:, (b + 1) * pulses : (b + 2) * pulses, :].reshape(total, RB)
            doppler[b + 1] += dot(ahead[1], x)
        for b in range(max(c * chunk - 1, 0), (c + 1) * chunk - (c < chunks - 1)):
            focus(b)

    for c in range(chunks + 1):

        def leave(k, carry):
            remote(c, lax.rem(me + k, ranks), me).wait_send()
            return carry

        lax.fori_loop(1, ranks, leave, 0)


def local(echoes, range_reference, kernels, shifts, phase_index, centroid, azimuth_reference):
    ranks = lax.axis_size("range")
    pulses, samples = echoes.shape[1:]
    second = samples // R1
    blocks = R1 // ranks
    total = ranks * pulses
    taps = kernels.shape[1]
    mats = np.stack([
        left_matrix(roots(R1, -1.0)),
        right_matrix(roots(second, -1.0)),
        right_matrix(roots(second, 1.0)),
        left_matrix(roots(R1, 1.0)),
    ])
    tables = np.concatenate([
        pair(twist(R1, second, -1.0) / math.sqrt(samples)),
        pair(twist(R1, second, 1.0) / math.sqrt(samples)),
    ])
    turn = azimuth_matrix(ranks, pulses)
    ahead = left_matrix(turn).reshape(2 * total, 2, ranks, 2, pulses // 2).transpose(3, 0, 2, 1, 4)
    ahead = ahead.reshape(2, 2 * total, total)
    back = left_matrix(turn.conj().T)
    vmem = pl.BlockSpec(memory_space=pltpu.VMEM)
    anywhere = pl.BlockSpec(memory_space=pl.ANY)
    dma = pltpu.SemaphoreType.DMA
    chunk = max(1, blocks // 4)
    focused = pl.pallas_call(
        functools.partial(turn_kernel, ranks, math.gcd(pulses // 2, 4), chunk),
        out_shape=jax.ShapeDtypeStruct((2 * total, blocks * RB), BF16),
        in_specs=[anywhere] * 9 + [pl.BlockSpec(memory_space=pltpu.SMEM)],
        out_specs=vmem,
        scratch_shapes=[
            pltpu.VMEM((2, R1 * pulses, RB), F32),
            pltpu.VMEM((2, R1 * pulses, RB), F32),
            pltpu.VMEM((2, R1, second), F32),
            pltpu.VMEM((ranks, blocks * pulses, RB), BF16),
            pltpu.VMEM((ranks, (blocks + 1) * pulses, RB), BF16),
            pltpu.VMEM((ranks, blocks * pulses, RB), BF16),
            pltpu.VMEM((ranks, (blocks + 1) * pulses, RB), BF16),
            pltpu.VMEM((blocks + 2, 2 * total, RB), F32),
            pltpu.VMEM((blocks, taps, total, RB), F32),
            pltpu.VMEM((blocks, 2, total, RB), F32),
            pltpu.VMEM((blocks, total, RB), jnp.int32),
            pltpu.VMEM(echoes.shape, BF16),
            pltpu.VMEM(range_reference.shape, F32),
            pltpu.VMEM(tables.shape, F32),
            pltpu.VMEM(mats.shape, BF16),
            pltpu.VMEM(kernels.shape[::-1], F32),
            pltpu.VMEM(shifts.shape, jnp.int32),
            pltpu.VMEM(shifts.shape, jnp.int32),
            pltpu.VMEM(azimuth_reference.shape, F32),
            pltpu.VMEM(ahead.shape, BF16),
            dma((11,)),
            dma((blocks // chunk + 1, ranks)),
            dma((blocks // chunk + 1, ranks)),
        ],
        compiler_params=pltpu.CompilerParams(
            vmem_limit_bytes=VMEM_BYTES, collective_id=0, has_side_effects=True
        ),
        name="turn_and_azimuth",
    )(
        echoes, range_reference, tables, mats, kernels.T, shifts, phase_index, azimuth_reference,
        ahead, centroid,
    )
    return dot(back, focused).astype(BF16).reshape(2, total, blocks * RB)


def solution(mesh):
    in_specs = (
        P("groups", "range", None),
        P(),
        P(),
        P("range", None),
        P("range", None),
        P("range"),
        P(None, "range", None),
    )
    out_specs = P("groups", None, "range")
    return jax.shard_map(local, mesh=mesh, in_specs=in_specs, out_specs=out_specs, check_vma=False)
```

```python
import functools
import math

import jax
import jax.numpy as jnp
import ml_dtypes
import numpy as np
from jax import lax
from jax.experimental import pallas as pl
from jax.experimental.pallas import tpu as pltpu
from jax.sharding import PartitionSpec as P

R1 = 128
RB = 128
F32 = jnp.float32
BF16 = jnp.bfloat16
VMEM_BYTES = 58 << 20


def roots(length, orient):
    line = np.arange(length)
    angles = 2.0 * math.pi / length * (line[:, None] * line[None, :] % length)
    rounded = lambda part: part.astype(ml_dtypes.bfloat16).astype(np.float64)
    return rounded(np.cos(angles)) + 1j * orient * rounded(np.sin(angles))


def twist(first_len, second_len, orient):
    whole = first_len * second_len
    turns = np.arange(first_len)[:, None] * np.arange(second_len)[None, :] % whole
    return np.exp(orient * 2j * math.pi / whole * turns)


def left_matrix(m):
    return np.block([[m.real, -m.imag], [m.imag, m.real]]).astype(ml_dtypes.bfloat16)


def right_matrix(m):
    return np.block([[m.real, m.imag], [-m.imag, m.real]]).astype(ml_dtypes.bfloat16)


def pair(m):
    return np.stack([m.real, m.imag]).astype(np.float32)


def azimuth_matrix(first, second):
    parts = np.einsum(
        "ka,mk,bm->bkam", roots(first, -1.0), twist(second, first, -1.0), roots(second, -1.0)
    )
    return parts.reshape(first * second, first * second) / math.sqrt(first * second)


def dot(a, b):
    return jnp.dot(a, b, preferred_element_type=F32)


def fetch(pairs, sems):
    copies = [pltpu.make_async_copy(src, dst, sems.at[i]) for i, (src, dst) in enumerate(pairs)]
    for copy in copies:
        copy.start()
    return copies


def turn_kernel(
    ranks, group, sizes, e_hbm, ref_hbm, tables_hbm, mats_hbm,
    kernels_hbm, shift_hbm, phase_hbm, az_hbm, ahead_hbm, centroid_ref,
    out_ref, lines, cells, slots, early_send, late_send, early_got, late_got,
    doppler, weights, filters, moves, e_ref, ref_ref, tables, mats,
    kernels_ref, shift_ref, phase_ref, az_ref, ahead, sems, send_sems, got_sems,
):
    me = lax.axis_index("range")
    blocks, total = shift_ref.shape
    pulses = total // ranks
    taps, phases = kernels_ref.shape
    lead = taps // 2 - 1
    chunks = len(sizes)
    starts = [sum(sizes[:c]) for c in range(chunks + 1)]

    barrier = pltpu.get_barrier_semaphore()

    def greet(k, carry):
        pl.semaphore_signal(
            barrier, inc=1, device_id={"range": lax.rem(me + k, ranks)},
            device_id_type=pl.DeviceIdType.MESH,
        )
        return carry

    lax.fori_loop(1, ranks, greet, 0)
    copies = fetch(
        [
            (e_hbm, e_ref), (ref_hbm, ref_ref), (tables_hbm, tables), (mats_hbm, mats),
            (kernels_hbm, kernels_ref), (shift_hbm, shift_ref), (phase_hbm, phase_ref),
            (az_hbm, az_ref), (ahead_hbm, ahead),
        ],
        sems,
    )
    part_pulses = pulses // 2

    copies[1].wait()
    for part in range(2):
        for k2 in range(ref_ref.shape[1] // R1):
            slots[part, k2 : k2 + 1, :] = ref_ref[part : part + 1, k2 * R1 : (k2 + 1) * R1]
    for part in range(2):
        slots[part] = slots[part].T
    for copy in (copies[2], copies[3], copies[0]):
        copy.wait()

    def spread(h):
        def one(n1, carry):
            lane = pl.multiple_of(n1 * RB, RB)
            for part in range(2):
                tile = e_ref[part, :, pl.ds(lane, RB)].astype(F32)
                lines[part, pl.ds(h * part_pulses * R1 + n1, part_pulses, stride=R1), :] = tile[
                    h * part_pulses : (h + 1) * part_pulses
                ]
            return carry

        lax.fori_loop(0, R1, one, 0, unroll=32)

    def times(re, im, tr, ti):
        return (re * tr - im * ti).astype(BF16), (re * ti + im * tr).astype(BF16)

    def step(g, carry):
        def line(part, j):
            return lines[part, pl.ds((g * group + j) * R1, R1), :].astype(BF16)

        x = jnp.concatenate(
            [jnp.concatenate([line(part, j) for j in range(group)], 1) for part in range(2)], 0
        )
        u = dot(mats[0], x)
        tr, ti = tables[0], tables[1]
        u = jnp.concatenate(
            [
                jnp.concatenate(
                    times(u[:R1, j * RB : (j + 1) * RB], u[R1:, j * RB : (j + 1) * RB], tr, ti), 1
                )
                for j in range(group)
            ],
            0,
        )
        s = dot(u, mats[1])
        tr, ti = slots[0], slots[1]
        s = jnp.concatenate(
            [
                jnp.concatenate(
                    times(s[j * R1 : (j + 1) * R1, :RB], s[j * R1 : (j + 1) * R1, RB:], tr, ti), 1
                )
                for j in range(group)
            ],
            0,
        )
        v = dot(s, mats[2])
        tr, ti = tables[2], tables[3]
        v = jnp.concatenate(
            [
                jnp.concatenate(
                    times(v[j * R1 : (j + 1) * R1, :RB], v[j * R1 : (j + 1) * R1, RB:], tr, ti), 0
                )
                for j in range(group)
            ],
            1,
        )
        r = dot(mats[3], v)
        for j in range(group):
            for part in range(2):
                cells[part, pl.ds(g * group + j, R1, stride=pulses), :] = r[
                    part * R1 : (part + 1) * R1, j * RB : (j + 1) * RB
                ]
        return carry

    def transform(h):
        spread(h)
        steps = part_pulses // group
        for g in range(h * steps, (h + 1) * steps):
            step(g, 0)

    def pack(h, d, b):
        begin = (d * blocks + b) * pulses + h * part_pulses
        return jnp.concatenate(
            [cells[part, pl.ds(begin, part_pulses), :] for part in range(2)], 0
        ).astype(BF16)

    def rows(c):
        if c == 1:
            return pl.ds(0, pulses + sizes[0] * pulses)
        return pl.ds(pulses + starts[c - 1] * pulses, sizes[c - 1] * pulses)

    def remote(c, to, owner):
        if c == 0:
            src, dst = early_send.at[to], early_got.at[owner]
        else:
            src, dst = late_send.at[to, rows(c)], late_got.at[owner, rows(c)]
        return pltpu.make_async_remote_copy(
            src_ref=src,
            dst_ref=dst,
            send_sem=send_sems.at[c, to],
            recv_sem=got_sems.at[c, owner],
            device_id={"range": to},
            device_id_type=pl.DeviceIdType.MESH,
        )

    half = ranks // 2
    side = me // half

    def depart(c):
        def across(k, carry):
            remote(c, (1 - side) * half + lax.rem(me + k, half), me).start()
            return carry

        def near(k, carry):
            remote(c, side * half + lax.rem(me + k, half), me).start()
            return carry

        lax.fori_loop(0, half, across, 0)
        lax.fori_loop(1, half, near, 0)

    transform(0)
    for d in range(ranks):
        for b in range(blocks):
            early_send[d, b * pulses : (b + 1) * pulses, :] = pack(0, d, b)
    pl.semaphore_wait(barrier, ranks - 1)
    depart(0)
    own_early = pltpu.make_async_copy(early_send.at[me], early_got.at[me], sems.at[9])
    own_early.start()
    transform(1)
    spot = lax.broadcasted_iota(jnp.int32, (pulses, RB), 1)
    mine = (spot < RB // 4) | (spot >= RB - RB // 4)
    zero = jnp.zeros((pulses, RB), F32)
    for d in range(ranks):
        packed = []
        for part in range(2):
            after = zero if d == ranks - 1 else cells[part, pl.ds((d + 1) * blocks * pulses, pulses), :]
            before = zero if d == 0 else cells[part, pl.ds((d * blocks - 1) * pulses, pulses), :]
            packed.append(jnp.where(spot < RB // 2, after, before))
        late_send[d, :pulses, :] = jnp.where(
            mine, packed[0], pltpu.roll(packed[1], RB // 2, 1)
        ).astype(BF16)
        for b in range(blocks):
            late_send[d, (b + 1) * pulses : (b + 2) * pulses, :] = pack(1, d, b)
    own_late = pltpu.make_async_copy(late_send.at[me], late_got.at[me], sems.at[10])
    own_late.start()
    for c in range(1, min(3, chunks) + 1):
        depart(c)
    for copy in copies[4:]:
        copy.wait()

    wide = lax.broadcasted_iota(jnp.int32, (blocks, 1), 0)
    turns = jnp.zeros((blocks, 1), jnp.int32)
    for b in range(blocks):
        turns = jnp.where(wide == b, centroid_ref[b], turns)
    turns = jnp.broadcast_to(turns, (blocks, total))
    lines = []
    for part in range(2):
        line = az_ref[part]
        step = 1
        while step < total:
            line = jnp.where((turns & step) != 0, pltpu.roll(line, step, 1), line)
            step *= 2
        lines.append(line)
    lines.append(shift_ref[...].astype(F32))
    lines.append(phase_ref[...].astype(F32))
    lines.append(jnp.zeros((RB - 4 * blocks, total), F32))
    columns = jnp.concatenate(lines, 0).T

    def column(j):
        return jnp.broadcast_to(columns[:, j : j + 1], (total, RB))

    left = jnp.concatenate([kernels_ref[...], jnp.zeros((taps, RB - phases), F32)], 1).T
    terms = []
    for _ in range(3):
        term = left.astype(BF16)
        left = left - term.astype(F32)
        terms.append(term[:phases])
    terms.append(jnp.zeros((RB - 3 * phases, taps), BF16))
    table = jnp.concatenate(terms, 0).astype(F32)
    table = jnp.concatenate(
        [jnp.broadcast_to(table[:, t : t + 1], (RB, RB)) for t in range(taps)], 1
    ).astype(BF16)
    slot = lax.broadcasted_iota(jnp.int32, (total, RB), 1)
    slot = jnp.where(slot < 3 * phases, lax.rem(slot, phases), -1)

    for b in range(blocks):
        filters[b, 0] = column(b)
        filters[b, 1] = column(blocks + b)
        moves[b] = column(2 * blocks + b).astype(jnp.int32)
        chosen = jnp.where(column(3 * blocks + b).astype(jnp.int32) == slot, 1.0, 0.0).astype(BF16)
        for t in range(0, taps, 2):
            pair_of = dot(chosen, table[:, t * RB : (t + 2) * RB])
            weights[b, t] = pair_of[:, :RB]
            weights[b, t + 1] = pair_of[:, RB:]

    size = 32
    lane = lax.broadcasted_iota(jnp.int32, (size, RB), 1)

    def focus(b):
        for row in range(0, total, size):
            here = pl.ds(row, size)
            shift = moves[b, here, :]
            where = (lane + shift + (RB - lead)) & (RB - 1)
            early = lane < RB - shift
            found = []
            for part in range(2):
                at = pl.ds(part * total + row, size)
                prev, cur, after = doppler[b, at, :], doppler[b + 1, at, :], doppler[b + 2, at, :]
                a = jnp.take_along_axis(jnp.where(lane >= RB - lead, prev, cur), where, axis=1)
                z = jnp.take_along_axis(jnp.where(lane >= RB - lead, cur, after), where, axis=1)
                x = jnp.where(early, a, z)
                summed = weights[b, 0, here, :] * x
                for t in range(1, taps):
                    summed += weights[b, t, here, :] * pltpu.roll(jnp.where(lane < t, z, x), RB - t, 1)
                found.append(summed)
            ar, ai = filters[b, 0, here, :], filters[b, 1, here, :]
            cells = pl.ds(b * RB, RB)
            out_ref[here, cells] = (found[0] * ar - found[1] * ai).astype(BF16)
            out_ref[pl.ds(total + row, size), cells] = (found[0] * ai + found[1] * ar).astype(BF16)

    def arrive(c):
        def one(k, carry):
            remote(c, me, lax.rem(me + k, ranks)).wait_recv()
            return carry

        lax.fori_loop(1, ranks, one, 0)

    own_early.wait()
    own_late.wait()
    arrive(0)
    for b in range(blocks):
        x = early_got[:, b * pulses : (b + 1) * pulses, :].reshape(total, RB)
        doppler[b + 1] = dot(ahead[0], x)
    for c in range(chunks):
        arrive(c + 1)
        if c + 3 < chunks:
            depart(c + 4)
        if c == 0:
            halo = late_got[:, :pulses, :].astype(F32)
            turned = jnp.concatenate([halo[:, :, RB // 2 :], halo[:, :, : RB // 2]], 2)
            edge = jnp.zeros((2 * total, RB), F32)
            for h in range(2):
                at = slice(h * part_pulses, (h + 1) * part_pulses)
                x = jnp.concatenate([halo[:, at], turned[:, at]], 1).astype(BF16)
                edge += dot(ahead[h], x.reshape(total, RB))
            doppler[0] = edge
            doppler[blocks + 1] = edge
        for b in range(starts[c], starts[c + 1]):
            x = late_got[:, (b + 1) * pulses : (b + 2) * pulses, :].reshape(total, RB)
            doppler[b + 1] += dot(ahead[1], x)
        for b in range(max(starts[c] - 1, 0), starts[c + 1] - (c < chunks - 1)):
            focus(b)

    for c in range(chunks + 1):

        def leave(k, carry):
            remote(c, lax.rem(me + k, ranks), me).wait_send()
            return carry

        lax.fori_loop(1, ranks, leave, 0)


def local(echoes, range_reference, kernels, shifts, phase_index, centroid, azimuth_reference):
    ranks = lax.axis_size("range")
    pulses, samples = echoes.shape[1:]
    second = samples // R1
    blocks = R1 // ranks
    total = ranks * pulses
    taps = kernels.shape[1]
    mats = np.stack([
        left_matrix(roots(R1, -1.0)),
        right_matrix(roots(second, -1.0)),
        right_matrix(roots(second, 1.0)),
        left_matrix(roots(R1, 1.0)),
    ])
    tables = np.concatenate([
        pair(twist(R1, second, -1.0) / math.sqrt(samples)),
        pair(twist(R1, second, 1.0) / math.sqrt(samples)),
    ])
    turn = azimuth_matrix(ranks, pulses)
    ahead = left_matrix(turn).reshape(2 * total, 2, ranks, 2, pulses // 2).transpose(3, 0, 2, 1, 4)
    ahead = ahead.reshape(2, 2 * total, total)
    back = left_matrix(turn.conj().T)
    vmem = pl.BlockSpec(memory_space=pltpu.VMEM)
    anywhere = pl.BlockSpec(memory_space=pl.ANY)
    dma = pltpu.SemaphoreType.DMA
    rest = blocks - 1
    parts = min(3, rest)
    sizes = tuple(rest // parts + (i < rest % parts) for i in range(parts)) + (1,)
    focused = pl.pallas_call(
        functools.partial(turn_kernel, ranks, math.gcd(pulses // 2, 4), sizes),
        out_shape=jax.ShapeDtypeStruct((2 * total, blocks * RB), BF16),
        in_specs=[anywhere] * 9 + [pl.BlockSpec(memory_space=pltpu.SMEM)],
        out_specs=vmem,
        scratch_shapes=[
            pltpu.VMEM((2, R1 * pulses, RB), F32),
            pltpu.VMEM((2, R1 * pulses, RB), F32),
            pltpu.VMEM((2, R1, second), F32),
            pltpu.VMEM((ranks, blocks * pulses, RB), BF16),
            pltpu.VMEM((ranks, (blocks + 1) * pulses, RB), BF16),
            pltpu.VMEM((ranks, blocks * pulses, RB), BF16),
            pltpu.VMEM((ranks, (blocks + 1) * pulses, RB), BF16),
            pltpu.VMEM((blocks + 2, 2 * total, RB), F32),
            pltpu.VMEM((blocks, taps, total, RB), F32),
            pltpu.VMEM((blocks, 2, total, RB), F32),
            pltpu.VMEM((blocks, total, RB), jnp.int32),
            pltpu.VMEM(echoes.shape, BF16),
            pltpu.VMEM(range_reference.shape, F32),
            pltpu.VMEM(tables.shape, F32),
            pltpu.VMEM(mats.shape, BF16),
            pltpu.VMEM(kernels.shape[::-1], F32),
            pltpu.VMEM(shifts.shape, jnp.int32),
            pltpu.VMEM(shifts.shape, jnp.int32),
            pltpu.VMEM(azimuth_reference.shape, F32),
            pltpu.VMEM(ahead.shape, BF16),
            dma((11,)),
            dma((len(sizes) + 1, ranks)),
            dma((len(sizes) + 1, ranks)),
        ],
        compiler_params=pltpu.CompilerParams(
            vmem_limit_bytes=VMEM_BYTES, collective_id=0, has_side_effects=True
        ),
        name="turn_and_azimuth",
    )(
        echoes, range_reference, tables, mats, kernels.T, shifts, phase_index, azimuth_reference,
        ahead, centroid,
    )
    return dot(back, focused).astype(BF16).reshape(2, total, blocks * RB)


def solution(mesh):
    in_specs = (
        P("groups", "range", None),
        P(),
        P(),
        P("range", None),
        P("range", None),
        P("range"),
        P(None, "range", None),
    )
    out_specs = P("groups", None, "range")
    return jax.shard_map(local, mesh=mesh, in_specs=in_specs, out_specs=out_specs, check_vma=False)
```
